256 devices in a mesh: seq: 64 (over x_hi, z, y), fsdp: 4 (over x_lo, core).
Axes of the slice: x: 4 (x_hi: 2, x_lo: 2; x = x_hi * 2 + x_lo), y: 4, z: 8, core: 2. Of those that a mesh axis runs over, the one named last changes fastest.
Arguments:
- query_t: bfloat16 [2560, 8192], P('fsdp', 'seq'), may hold values from -6 to 6
- key_head_rows: bfloat16 [512, 8192], P('fsdp', 'seq'), may hold values from -6 to 6
- value_head_rows: bfloat16 [512, 8192], P('fsdp', 'seq'), may hold values from -6 to 6
- attn_out: bfloat16 [2560, 8192], P('fsdp', 'seq'), may hold values from -6 to 6
- lse: bfloat16 [20, 8192], P('fsdp', 'seq'), may hold values from 3 to 8
- out_grad_t: bfloat16 [5120, 8192], P('fsdp', 'seq'), may hold values from -6 to 6
- out_weight: bfloat16 [5120, 2560], P('fsdp'), may hold values from -0.125 to 0.125
- parents: int32 [64], replicated, may hold values from -1 to 62, as said below
- node_of: int32 [64], replicated, may hold values from 0 to 63, each once
Outputs:
- query_grad: float32 [2560, 8192], P('fsdp', 'seq')
- key_gradient: float32 [512, 8192], P('fsdp', 'seq')
- value_gradient: float32 [512, 8192], P('fsdp', 'seq')
The draws below stay inside these ranges and needn't reach their ends.
Inputs may be any that keep to these rules, and one draw needn't show every extreme that they name: parents[0] = -1; for every node n > 0, parents[n] lies in 0 to n - 1, and parents[63] = 62. Stored block s of the sequence holds trie node node_of[s]; every node is held once.
All inputs are finite; a program needn't handle non-finite values.
Results may differ from the reference program's by a relative error of at most 0.022.
Values may be sent and summed in bfloat16 or wider, within the bound.
A program may use at most 128 MiB of HBM per device.

```python
import jax
import jax.numpy as jnp
from jax import lax

D = 5120
HEAD_SIZE = 128
QUERY_GROUP = 5
KEY_VALUE_HEADS = 4
HQ = 20
BLK = 128
PACKED_TOKENS = 8192
NBLK = 64


def draw_parents(key, part):
    key = jax.random.fold_in(key, 11)
    coin_key, jump_key = jax.random.split(key)
    node_ids = jnp.arange(NBLK, dtype=jnp.int32)
    coins = jax.random.randint(coin_key, (NBLK,), 0, 8)
    jumps = jax.random.randint(jump_key, (NBLK,), 0, jnp.maximum(node_ids, 1))
    chosen = jnp.where(coins < 5, node_ids - 1, jumps)
    chosen = jnp.where(node_ids == NBLK - 1, NBLK - 2, chosen)
    chosen = jnp.where(node_ids == 0, -1, chosen)
    return chosen.astype(jnp.int32)


def spiked(values, key, source, target, parts, factor):
    owner, partner = [(jnp.arange(values.shape[axis_at]) // (values.shape[axis_at] // parts)).reshape([-1 if axis == axis_at else 1 for axis in range(values.ndim)]) for axis_at in (source, target)]
    chosen = jax.random.permutation(key, parts)[partner]
    strong = (owner == chosen) | (owner == (partner + parts // 2) % parts)
    return jnp.where(strong, factor * values, values)


def steps_of(rng, shape, pieces, least, largest):
    level, own = 1.0, jax.random.fold_in(rng, 6)
    for dim, parts in pieces:
        heights = jnp.exp(jax.random.uniform(jax.random.fold_in(own, dim), (parts,), jnp.float32, least / len(pieces), largest / len(pieces)))
        level = level * jnp.repeat(heights, shape[dim] // parts).reshape([-1 if axis == dim else 1 for axis in range(len(shape))])
    return level


def bell_draw(stream_key, extent, scale, bound, cuts=(), held_as=jnp.bfloat16):
    array = jax.random.normal(stream_key, extent, jnp.float32) * scale
    if len(cuts) > 0:
        array = steps_of(stream_key, extent, cuts, -0.22, 0.18) * array
    return jnp.clip(array, min=-bound, max=bound).astype(held_as)


def bell_draw_with(own_key, dims, spread, most, shards, heavy, kind=jnp.bfloat16):
    result = spread * jax.random.normal(own_key, dims, jnp.float32)
    if shards:
        result = result * steps_of(own_key, dims, shards, -0.22, 0.18)
    return jnp.clip(spiked(result, jax.random.fold_in(own_key, 3), *heavy), -most, most).astype(kind)


def setup_inputs(seed: int = 0) -> dict:
    key_of = jax.random.split(jax.random.key(seed), 10)
    return {
        "query_t": bell_draw(key_of[0], (HQ * HEAD_SIZE, PACKED_TOKENS), 1.0, 6.0, ((0, 4), (1, 64))),
        "key_head_rows": bell_draw(key_of[1], (KEY_VALUE_HEADS * HEAD_SIZE, PACKED_TOKENS), 1.0, 6.0, ((0, 4), (1, 64))),
        "value_head_rows": bell_draw(key_of[2], (KEY_VALUE_HEADS * HEAD_SIZE, PACKED_TOKENS), 1.0, 6.0, ((0, 4), (1, 64))),
        "attn_out": bell_draw(key_of[3], (HQ * HEAD_SIZE, PACKED_TOKENS), 1.0, 6.0, ((0, 4), (1, 64))),
        "lse": jnp.clip(3.0 + 5.0 * jax.random.uniform(key_of[4], (HQ, PACKED_TOKENS), jnp.float32) ** steps_of(key_of[4], (HQ, PACKED_TOKENS), ((0, 4), (1, 64)), -0.2, 0.2), 3.0, 8.0).astype(jnp.bfloat16),
        "out_grad_t": bell_draw(key_of[5], (D, PACKED_TOKENS), 1.0, 6.0, ((0, 4), (1, 64))),
        "out_weight": bell_draw_with(key_of[6], (D, HQ * HEAD_SIZE), D ** -0.5, 0.125, ((0, 4),), (0, 1, 4, 2.0)),
        "parents": draw_parents(jax.random.fold_in(key_of[9], 71), 0),
        "node_of": jax.random.permutation(key_of[8], NBLK).astype(jnp.int32),
    }


def ancestry(parents, node_of):
    node_count = parents.shape[0]
    node_ids = jnp.arange(node_count, dtype=jnp.int32)
    reaches = (parents[:, None] == node_ids[None, :]).astype(jnp.int32) + jnp.eye(node_count, dtype=jnp.int32)
    for repeat_idx in range(node_count.bit_length()):
        reaches = (jnp.dot(reaches, reaches) > 0).astype(jnp.int32)
    placed = (node_of[:, None] == node_ids[None, :]).astype(jnp.int32)
    return jnp.dot(jnp.dot(placed, reaches), placed.T)


def reference(query_t, key_head_rows, value_head_rows, attn_out, lse, out_grad_t, out_weight, parents, node_of):
    score_scale = HEAD_SIZE ** -0.5
    attn_grad = jnp.dot(out_weight.T, out_grad_t, preferred_element_type=jnp.float32).astype(jnp.bfloat16)
    delta = jnp.sum((attn_grad.astype(jnp.float32) * attn_out.astype(jnp.float32)).reshape(HQ, HEAD_SIZE, PACKED_TOKENS), axis=1).astype(jnp.bfloat16)
    visible = ancestry(parents, node_of)
    positions = jnp.arange(PACKED_TOKENS, dtype=jnp.int32)
    blocks = positions // BLK
    allowed = (visible[blocks][:, blocks] > 0) & ((blocks[:, None] != blocks[None, :]) | (positions[None, :] <= positions[:, None]))

    def per_head(head):
        kv_head = head // QUERY_GROUP
        queries = lax.dynamic_slice_in_dim(query_t, head * HEAD_SIZE, HEAD_SIZE, 0)
        grads = lax.dynamic_slice_in_dim(attn_grad, head * HEAD_SIZE, HEAD_SIZE, 0)
        key_rows = lax.dynamic_slice_in_dim(key_head_rows, kv_head * HEAD_SIZE, HEAD_SIZE, 0)
        value_rows = lax.dynamic_slice_in_dim(value_head_rows, kv_head * HEAD_SIZE, HEAD_SIZE, 0)
        shifts = lax.dynamic_slice_in_dim(lse, head, 1, 0)[0].astype(jnp.float32)
        centre = lax.dynamic_slice_in_dim(delta, head, 1, 0)[0].astype(jnp.float32)
        scores = jnp.dot(queries.T, key_rows, preferred_element_type=jnp.float32) * score_scale
        probs = jnp.where(allowed, jnp.exp(scores - shifts[:, None]), 0.0)
        weights = probs.astype(jnp.bfloat16)
        dprob = jnp.dot(grads.T, value_rows, preferred_element_type=jnp.float32)
        dscore = (probs * (dprob - centre[:, None]) * score_scale).astype(jnp.bfloat16)
        q_grad = jnp.dot(key_rows, dscore.T, preferred_element_type=jnp.float32)
        k_grad = jnp.dot(queries, dscore, preferred_element_type=jnp.float32)
        v_grad = jnp.dot(grads, weights, preferred_element_type=jnp.float32)
        return q_grad, k_grad, v_grad

    q_all, key_matrix, value_matrix = lax.map(per_head, jnp.arange(HQ, dtype=jnp.int32))
    query_grad = q_all.reshape(HQ * HEAD_SIZE, PACKED_TOKENS)
    key_gradient = jnp.sum(key_matrix.reshape(KEY_VALUE_HEADS, QUERY_GROUP, HEAD_SIZE, PACKED_TOKENS), axis=1).reshape(KEY_VALUE_HEADS * HEAD_SIZE, PACKED_TOKENS)
    value_gradient = jnp.sum(value_matrix.reshape(KEY_VALUE_HEADS, QUERY_GROUP, HEAD_SIZE, PACKED_TOKENS), axis=1).reshape(KEY_VALUE_HEADS * HEAD_SIZE, PACKED_TOKENS)
    return (query_grad, key_gradient, value_gradient)
```

```python
import jax
import jax.numpy as jnp
from jax import lax
from jax.experimental import pallas as pl
from jax.experimental.pallas import tpu as pltpu
from jax.sharding import PartitionSpec as P

MESH = pl.DeviceIdType.MESH
HD = 128
BLK = 128
GRP = 5
ROWS = GRP * HD
NX, NZ, NY = 2, 8, 4
NODES = NX * NZ * NY
PACK = ROWS + 16
CUT_Q, CUT_G = 320, 336
SCALE = HD**-0.5
F32, BF16 = jnp.float32, jnp.bfloat16
ANY = pl.BlockSpec(memory_space=pl.ANY)
VMEM = pl.BlockSpec(memory_space=pltpu.VMEM)


def where_am_i():
    s, f = lax.axis_index("seq"), lax.axis_index("fsdp")
    xh, z, y = s // (NZ * NY), (s // NY) % NZ, s % NY
    at = lambda xh, z, y: (xh * NZ + z) * NY + y
    return dict(
        s=s,
        f=f,
        xl=f // 2,
        core=f % 2,
        xh=xh,
        z=z,
        y=y,
        yp=(at(xh, z, (y + 1) % NY), f),
        ym=(at(xh, z, (y + NY - 1) % NY), f),
        zp=(at(xh, (z + 1) % NZ, y), f),
        zm=(at(xh, (z + NZ - 1) % NZ, y), f),
        xo=(at(1 - xh, z, y), f),
    )


def greet(partners):
    barrier = pltpu.get_barrier_semaphore()
    for partner in partners:
        pl.semaphore_signal(barrier, inc=1, device_id=partner, device_id_type=MESH)
    pl.semaphore_wait(barrier, len(partners))


class Wires:
    def __init__(self, send_sems, recv_sems):
        self.send_sems, self.recv_sems, self.count, self.sent = send_sems, recv_sems, 0, []

    def send(self, src, dst, to, landing=None):
        copy = pltpu.make_async_remote_copy(
            src_ref=src,
            dst_ref=dst,
            send_sem=self.send_sems.at[self.count],
            recv_sem=self.recv_sems.at[self.count],
            device_id=to,
            device_id_type=MESH,
        )
        self.count += 1
        copy.start()
        self.sent.append(copy)
        return copy.wait_recv

    def finish(self):
        for copy in self.sent:
            copy.wait_send()


def gather_kernel(
    q_ref, k_ref, v_ref, o_ref, lse_ref, g_ref, w_ref, par_ref, node_ref,
    q4, g4, kv, vis,
    g_buf, w_buf, o_buf, lse_buf, part, out_a, in_a, sum_b, in_b, out_c, in_c, pack,
    local_sems, send_sems, recv_sems,
):
    me = where_am_i()
    xl, core = me["xl"], me["core"]
    sib = (me["s"], 2 * xl + 1 - core)
    xlo = (me["s"], 2 * (1 - xl) + core)

    def fetch(src, dst, index):
        copy = pltpu.make_async_copy(src, dst, local_sems.at[index])
        copy.start()
        return copy

    get_g = fetch(g_ref, g_buf, 0)
    get_w = []
    for i, (a, b) in enumerate(((1 - xl, 1 - core), (1 - xl, core), (xl, 1 - core), (xl, core))):
        first = pl.multiple_of((2 * a + b) * ROWS, ROWS)
        get_w.append(fetch(w_ref.at[:, pl.ds(first, ROWS)], w_buf.at[i], 1 + i))
    get_k = fetch(k_ref, kv.at[0, 0, 0], 5)
    get_v = fetch(v_ref, kv.at[0, 0, 1], 6)
    get_q = fetch(q_ref, q4.at[0], 7)
    get_o = fetch(o_ref, o_buf, 8)
    get_lse = fetch(lse_ref, lse_buf, 9)

    greet([me["yp"], me["ym"], me["zp"], me["zm"], me["xo"], sib, xlo])
    wires = Wires(send_sems, recv_sems)

    got_xk = wires.send(k_ref, kv.at[0, 1, 0], me["xo"])
    got_xv = wires.send(v_ref, kv.at[0, 1, 1], me["xo"])
    got_q1 = wires.send(q_ref, q4.at[1], me["yp"])
    got_q3 = wires.send(q_ref, q4.at[3], me["ym"])

    get_g.wait()
    gt = g_buf[...].T

    def partial_sum(i):
        get_w[i].wait()
        return jnp.dot(gt, w_buf[i], preferred_element_type=F32)

    out_a[...] = partial_sum(0).astype(BF16)
    got_a = wires.send(out_a, in_a, sib)
    get_k.wait()
    get_v.wait()
    got_xk()
    got_xv()
    got_p = wires.send(kv.at[0], kv.at[1], me["zp"])
    got_m = wires.send(kv.at[0], kv.at[7], me["zm"])
    part[...] = partial_sum(1)
    got_a()
    sum_b[...] = (part[...] + in_a[...].astype(F32)).astype(BF16)
    got_b = wires.send(sum_b, in_b, xlo)
    out_c[...] = partial_sum(2).astype(BF16)
    got_c = wires.send(out_c, in_c, sib)
    part[...] = partial_sum(3)

    got_p()
    got_p = wires.send(kv.at[1], kv.at[2], me["zp"])
    got_m()
    got_m = wires.send(kv.at[7], kv.at[6], me["zm"])

    got_q1()
    got_q2a = wires.send(q4.at[1, pl.ds(0, CUT_Q)], q4.at[2, pl.ds(0, CUT_Q)], me["yp"])
    got_q3()
    got_q2b = wires.send(
        q4.at[3, pl.ds(CUT_Q, ROWS - CUT_Q)], q4.at[2, pl.ds(CUT_Q, ROWS - CUT_Q)], me["ym"]
    )

    rows = lax.broadcasted_iota(jnp.int32, (NODES, NODES), 0)
    cols = lax.broadcasted_iota(jnp.int32, (NODES, NODES), 1)
    reach = jnp.where((rows == par_ref[...]) | (rows == cols), 1.0, 0.0)
    for _ in range(NODES.bit_length()):
        reach = jnp.where(jnp.dot(reach, reach, preferred_element_type=F32) > 0.5, 1.0, 0.0)
    placed = jnp.where(rows == node_ref[...], 1.0, 0.0)
    k_row = lax.broadcasted_iota(jnp.int32, (NODES, 16), 1)
    k_all = lax.broadcasted_iota(jnp.int32, (NODES, 16), 0)
    k_xh = jnp.where(k_row >= NZ, 1 - me["xh"], me["xh"])
    k_z = (me["z"] + NZ - (k_row & (NZ - 1))) & (NZ - 1)
    pick_k = jnp.where(k_all == (k_xh * NZ + k_z) * NY + me["y"], 1.0, 0.0)
    q_col = lax.broadcasted_iota(jnp.int32, (NODES, 128), 1)
    q_all = lax.broadcasted_iota(jnp.int32, (NODES, 128), 0)
    q_at = (me["xh"] * NZ + me["z"]) * NY + ((me["y"] + NY - (q_col & (NY - 1))) & (NY - 1))
    pick_q = jnp.where((q_all == q_at) & (q_col < NY), 1.0, 0.0)
    node_k = jnp.dot(placed, pick_k, preferred_element_type=F32)
    node_q = jnp.dot(placed, pick_q, preferred_element_type=F32)
    above = jnp.dot(reach, node_q, preferred_element_type=F32)
    seen = lax.dot_general(node_k, above, (((0,), (0,)), ((), ())), preferred_element_type=F32)
    vis[...] = jnp.where(seen > 0.5, 1, 0)

    get_o.wait()
    get_lse.wait()
    got_c()
    got_b()
    grad = part[...] + in_c[...].astype(F32) + in_b[...].astype(F32)
    pack[pl.ds(ROWS, 16), :] = jnp.zeros((16, BLK), BF16)
    deltas = []
    for h in range(GRP):
        rows_h = pl.ds(h * HD, HD)
        grad_h = grad[:, h * HD : (h + 1) * HD].T.astype(BF16)
        pack[rows_h, :] = grad_h
        deltas.append(
            jnp.sum(grad_h.astype(F32) * o_buf[rows_h, :].astype(F32), axis=0, keepdims=True)
        )
    tail = jnp.concatenate(
        [lse_buf[...].astype(F32)] + deltas + [jnp.zeros((16 - 2 * GRP, BLK), F32)], axis=0
    )
    pack[pl.ds(ROWS, 16), :] = tail.astype(BF16)
    got_g1 = wires.send(pack, g4.at[1], me["yp"])
    got_g3 = wires.send(pack, g4.at[3], me["ym"])
    put_g = fetch(pack, g4.at[0], 10)

    got_p()
    got_p = wires.send(kv.at[2], kv.at[3], me["zp"])
    got_m()
    got_m = wires.send(kv.at[6], kv.at[5], me["zm"])
    got_p()
    got_p = wires.send(kv.at[3, 0], kv.at[4, 0], me["zp"])
    got_m()
    got_m = wires.send(kv.at[5, 1], kv.at[4, 1], me["zm"])

    got_g1()
    got_g2a = wires.send(g4.at[1, pl.ds(0, CUT_G)], g4.at[2, pl.ds(0, CUT_G)], me["yp"])
    got_g3()
    got_g2b = wires.send(
        g4.at[3, pl.ds(CUT_G, PACK - CUT_G)], g4.at[2, pl.ds(CUT_G, PACK - CUT_G)], me["ym"]
    )
    got_q2a()
    got_q2b()
    got_p()
    got_m()
    got_g2a()
    got_g2b()
    get_q.wait()
    put_g.wait()
    wires.finish()


def gather(q, k, v, o, lse, g, w, par, node):
    return pl.pallas_call(
        gather_kernel,
        out_shape=(
            jax.ShapeDtypeStruct((NY, ROWS, BLK), BF16),
            jax.ShapeDtypeStruct((NY, PACK, BLK), BF16),
            jax.ShapeDtypeStruct((NZ, NX, 2, HD, BLK), BF16),
            jax.ShapeDtypeStruct((NZ * NX, 128), jnp.int32),
        ),
        in_specs=[ANY] * 7 + [VMEM] * 2,
        out_specs=(ANY, ANY, ANY, VMEM),
        scratch_shapes=[
            pltpu.VMEM(g.shape, BF16),
            pltpu.VMEM((4, w.shape[0], ROWS), BF16),
            pltpu.VMEM((ROWS, BLK), BF16),
            pltpu.VMEM((GRP, BLK), BF16),
            pltpu.VMEM((BLK, ROWS), F32),
        ]
        + [pltpu.VMEM((BLK, ROWS), BF16)] * 6
        + [
            pltpu.VMEM((PACK, BLK), BF16),
            pltpu.SemaphoreType.DMA((11,)),
            pltpu.SemaphoreType.DMA((21,)),
            pltpu.SemaphoreType.DMA((21,)),
        ],
        compiler_params=pltpu.CompilerParams(
            collective_id=0, has_side_effects=True, vmem_limit_bytes=48 << 20
        ),
        name="gather_and_head_grads",
    )(q, k, v, o, lse, g, w, par, node)


def attend_kernel(vis, q4, g4, kv, dq, dkv, q_c, g_c, k_t, v_t, dq_acc, dkv_acc):
    dq_acc[...] = jnp.zeros_like(dq_acc)
    dkv_acc[...] = jnp.zeros_like(dkv_acc)
    ahead = lax.broadcasted_iota(jnp.int32, (BLK, BLK), 0) - lax.broadcasted_iota(
        jnp.int32, (BLK, BLK), 1
    )

    def flip(i, carry):
        zi, xi = i % NZ, i // NZ
        k_t[i] = kv[zi, xi, 0].T
        v_t[i] = kv[zi, xi, 1].T
        return carry

    lax.fori_loop(0, NZ * NX, flip, 0)

    for qi in range(NY):
        for h in range(GRP):
            q_c[:, pl.ds(h * BLK, BLK)] = q4[qi, pl.ds(h * HD, HD), :]
            g_c[:, pl.ds(h * BLK, BLK)] = g4[qi, pl.ds(h * HD, HD), :]
        tail = g4[qi, pl.ds(ROWS, 16), :].astype(F32)

        def pair(i, carry, qi=qi, tail=tail):
            @pl.when(vis[i, qi] > 0)
            def _():
                zi, xi = i % NZ, i // NZ
                limit = jnp.where((i == 0) & (qi == 0), 0, BLK)
                s_all = jnp.dot(k_t[i], q_c[...], preferred_element_type=F32)
                dp_all = jnp.dot(v_t[i], g_c[...], preferred_element_type=F32)
                w_parts, ds_parts = [], []
                for h in range(GRP):
                    cols = slice(h * BLK, (h + 1) * BLK)
                    lse_h = tail[h : h + 1, :]
                    delta_h = tail[GRP + h : GRP + h + 1, :]
                    p = jnp.exp(s_all[:, cols] * SCALE - lse_h)
                    p = jnp.where(ahead <= limit, p, 0.0)
                    w_parts.append(p.astype(BF16))
                    ds_parts.append((p * (dp_all[:, cols] - delta_h) * SCALE).astype(BF16))
                w_all = jnp.concatenate(w_parts, axis=1)
                ds_all = jnp.concatenate(ds_parts, axis=1)
                dq_t = jnp.dot(kv[zi, xi, 0], ds_all, preferred_element_type=F32)
                dq_acc[qi] += dq_t
                nt = (((1,), (1,)), ((), ()))
                dkv_acc[zi, xi, 0] += lax.dot_general(
                    q_c[...], ds_all, nt, preferred_element_type=F32
                )
                dkv_acc[zi, xi, 1] += lax.dot_general(
                    g_c[...], w_all, nt, preferred_element_type=F32
                )

            return carry

        lax.fori_loop(0, NZ * NX, pair, 0)
        for h in range(GRP):
            dq[qi, pl.ds(h * HD, HD), :] = dq_acc[qi, :, pl.ds(h * BLK, BLK)].astype(BF16)
    dkv[...] = dkv_acc[...].astype(BF16)


def attend(vis, q4, g4, kv):
    return pl.pallas_call(
        attend_kernel,
        out_shape=(
            jax.ShapeDtypeStruct((NY, ROWS, BLK), BF16),
            jax.ShapeDtypeStruct((NZ, NX, 2, HD, BLK), BF16),
        ),
        in_specs=[pl.BlockSpec(memory_space=pltpu.SMEM)] + [VMEM] * 3,
        out_specs=(VMEM, VMEM),
        scratch_shapes=[
            pltpu.VMEM((HD, ROWS), BF16),
            pltpu.VMEM((HD, ROWS), BF16),
            pltpu.VMEM((NZ * NX, BLK, HD), BF16),
            pltpu.VMEM((NZ * NX, BLK, HD), BF16),
            pltpu.VMEM((NY, HD, ROWS), F32),
            pltpu.VMEM((NZ, NX, 2, HD, BLK), F32),
        ],
        compiler_params=pltpu.CompilerParams(vmem_limit_bytes=48 << 20),
        name="attend_visible_pairs",
    )(vis, q4, g4, kv)


def scatter_kernel(
    dq, dkv, q_out, k_out, v_out,
    p_out, m_out, p_in, m_in, qp_out, qm_out, qp_half, qm_half, qp_in, qm_in, x_out, x_in,
    send_sems, recv_sems,
):
    me = where_am_i()
    greet([me["yp"], me["ym"], me["zp"], me["zm"], me["xo"]])
    wires = Wires(send_sems, recv_sems)
    low, high = pl.ds(0, CUT_Q), pl.ds(CUT_Q, ROWS - CUT_Q)

    def add(a, b):
        return a.astype(F32) + b.astype(F32)

    got_p = wires.send(dkv.at[4, 0], p_in.at[0, 0], me["zp"])
    got_m = wires.send(dkv.at[4, 1], m_in.at[0, 1], me["zm"])
    got_qp = wires.send(dq.at[2, low], qp_half, me["yp"])
    got_qm = wires.send(dq.at[2, high], qm_half, me["ym"])

    p_out[0, 1] = dkv[5, 1]
    m_out[0, 0] = dkv[3, 0]
    got_p()
    p_out[0, 0] = add(dkv[5, 0], p_in[0, 0]).astype(BF16)
    got_p = wires.send(p_out.at[0], p_in.at[1], me["zp"])
    got_m()
    m_out[0, 1] = add(dkv[3, 1], m_in[0, 1]).astype(BF16)
    got_m = wires.send(m_out.at[0], m_in.at[1], me["zm"])

    qp_out[high, :] = dq[3, high, :]
    qm_out[low, :] = dq[1, low, :]
    got_qp()
    qp_out[low, :] = add(dq[3, low, :], qp_half[...]).astype(BF16)
    got_qp = wires.send(qp_out, qp_in, me["yp"])
    got_qm()
    qm_out[high, :] = add(dq[1, high, :], qm_half[...]).astype(BF16)
    got_qm = wires.send(qm_out, qm_in, me["ym"])

    for step in (1, 2):
        got_p()
        p_out[step] = add(dkv[5 + step], p_in[step]).astype(BF16)
        got_p = wires.send(p_out.at[step], p_in.at[step + 1], me["zp"])
        got_m()
        m_out[step] = add(dkv[3 - step], m_in[step]).astype(BF16)
        got_m = wires.send(m_out.at[step], m_in.at[step + 1], me["zm"])

    got_qp()
    got_qm()
    q_out[...] = add(dq[0], qp_in[...]) + qm_in[...].astype(F32)
    got_p()
    got_m()
    x_out[...] = (add(dkv[0, 1], p_in[3, 1]) + m_in[3, 1].astype(F32)).astype(BF16)
    got_x = wires.send(x_out, x_in, me["xo"])
    own = add(dkv[0, 0], p_in[3, 0]) + m_in[3, 0].astype(F32)
    got_x()
    own = own + x_in[...].astype(F32)
    k_out[...] = own[0]
    v_out[...] = own[1]
    wires.finish()


def scatter(dq, dkv):
    pair = (NX, 2, HD, BLK)
    return pl.pallas_call(
        scatter_kernel,
        out_shape=(
            jax.ShapeDtypeStruct((ROWS, BLK), F32),
            jax.ShapeDtypeStruct((HD, BLK), F32),
            jax.ShapeDtypeStruct((HD, BLK), F32),
        ),
        in_specs=[VMEM] * 2,
        out_specs=(VMEM,) * 3,
        scratch_shapes=[
            pltpu.VMEM((3, *pair), BF16),
            pltpu.VMEM((3, *pair), BF16),
            pltpu.VMEM((4, *pair), BF16),
            pltpu.VMEM((4, *pair), BF16),
            pltpu.VMEM((ROWS, BLK), BF16),
            pltpu.VMEM((ROWS, BLK), BF16),
            pltpu.VMEM((CUT_Q, BLK), BF16),
            pltpu.VMEM((ROWS - CUT_Q, BLK), BF16),
            pltpu.VMEM((ROWS, BLK), BF16),
            pltpu.VMEM((ROWS, BLK), BF16),
            pltpu.VMEM((2, HD, BLK), BF16),
            pltpu.VMEM((2, HD, BLK), BF16),
            pltpu.SemaphoreType.DMA((13,)),
            pltpu.SemaphoreType.DMA((13,)),
        ],
        compiler_params=pltpu.CompilerParams(
            collective_id=1, has_side_effects=True, vmem_limit_bytes=48 << 20
        ),
        name="scatter_sums",
    )(dq, dkv)


def body(q, k, v, o, lse, g, w, parents, node_of):
    q4, g4, kv, vis = gather(q, k, v, o, lse, g, w, parents[None, :], node_of[None, :])
    dq, dkv = attend(vis, q4, g4, kv)
    return scatter(dq, dkv)


def solution(mesh):
    both, one = P("fsdp", "seq"), P()
    return jax.shard_map(
        body,
        mesh=mesh,
        in_specs=(both,) * 6 + (P("fsdp", None), one, one),
        out_specs=(both,) * 3,
        check_vma=False,
    )
```

```python
import math

import jax
import jax.numpy as jnp
from jax import lax
from jax.experimental import pallas as pl
from jax.experimental.pallas import tpu as pltpu
from jax.sharding import PartitionSpec as P

MESH = pl.DeviceIdType.MESH
HD = 128
BLK = 128
GRP = 5
ROWS = GRP * HD
NX, NZ, NY = 2, 8, 4
NODES = NX * NZ * NY
KEYS = NX * NZ
HALF = HD // 2
CUTS = ((0, 2), (2, GRP))
SCALE = HD**-0.5
LOG2E = math.log2(math.e)
F32, BF16 = jnp.float32, jnp.bfloat16
HBM = pl.BlockSpec(memory_space=pltpu.HBM)
VMEM = pl.BlockSpec(memory_space=pltpu.VMEM)
SMEM = pl.BlockSpec(memory_space=pltpu.SMEM)
NT = (((1,), (1,)), ((), ()))


def place(space, *arrays):
    return [pltpu.with_memory_space_constraint(array, space) for array in arrays]


def where_am_i():
    s, f = lax.axis_index("seq"), lax.axis_index("fsdp")
    xh, z, y = s // (NZ * NY), (s // NY) % NZ, s % NY
    at = lambda xh, z, y: (xh * NZ + z) * NY + y
    return dict(
        s=s,
        f=f,
        xl=f // 2,
        core=f % 2,
        xh=xh,
        z=z,
        y=y,
        yp=(at(xh, z, (y + 1) % NY), f),
        ym=(at(xh, z, (y + NY - 1) % NY), f),
        y2=(at(xh, z, (y + 2) % NY), f),
        zp=(at(xh, (z + 1) % NZ, y), f),
        zm=(at(xh, (z + NZ - 1) % NZ, y), f),
        xo=(at(1 - xh, z, y), f),
    )


def hail(partners):
    barrier = pltpu.get_barrier_semaphore()
    for partner in partners:
        pl.semaphore_signal(barrier, inc=1, device_id=partner, device_id_type=MESH)
    return lambda: pl.semaphore_wait(barrier, len(partners))


class Wires:
    def __init__(self, send_sems, recv_sems):
        self.send_sems, self.recv_sems, self.count, self.sent = send_sems, recv_sems, 0, []

    def send(self, src, dst, to):
        copy = pltpu.make_async_remote_copy(
            src_ref=src,
            dst_ref=dst,
            send_sem=self.send_sems.at[self.count],
            recv_sem=self.recv_sems.at[self.count],
            device_id=to,
            device_id_type=MESH,
        )
        self.count += 1
        copy.start()
        self.sent.append(copy)
        return copy.wait_recv

    def finish(self):
        for copy in self.sent:
            copy.wait_send()


def list_pairs(me, parents, node_of):
    iota = lambda shape, dim: lax.broadcasted_iota(jnp.int32, shape, dim)
    square = (NODES, NODES)
    rows, cols = iota(square, 0), iota(square, 1)
    hot = lambda mask: jnp.where(mask, 1.0, 0.0)
    dot = lambda a, b: jnp.dot(a, b, preferred_element_type=F32)
    reach = hot((rows == parents) | (rows == cols))
    for _ in range(NODES.bit_length()):
        reach = hot(dot(reach, reach) > 0.5)
    placed = hot(rows == node_of)
    k, q = cols % KEYS, cols // KEYS
    k_xh = jnp.where(k >= NZ, 1 - me["xh"], me["xh"])
    k_z = (me["z"] + NZ - k % NZ) % NZ
    q_y = (me["y"] + NY - q) % NY
    node_k = dot(placed, hot(rows == (k_xh * NZ + k_z) * NY + me["y"]))
    node_q = dot(placed, hot(rows == (me["xh"] * NZ + me["z"]) * NY + q_y))
    seen = jnp.sum(node_k * dot(reach, node_q), axis=0, keepdims=True)
    pair = iota((1, NODES), 1)
    seen = hot((seen > 0.5) & (pair > 0))
    rank = dot(seen, hot(rows < cols))
    spot = hot((rows.astype(F32) == rank) & (seen > 0.5))
    order = lax.dot_general(pair.astype(F32), spot, NT, preferred_element_type=F32)
    return order.astype(jnp.int32), jnp.sum(seen, axis=1, keepdims=True).astype(jnp.int32)


def gather_kernel(
    q_ref, k_ref, v_ref, o_ref, lse_ref, g_ref, w_ref, par_ref, node_ref,
    q4, g4, tail, kk, kt, vt, plan,
    g_buf, w_buf, o_buf, lse_buf, q_buf, v_buf, par_buf, node_buf,
    part, out_a, in_a, sum_b, in_b, out_c, in_c,
    local_sems, send_sems, recv_sems,
):
    me = where_am_i()
    xl, core = me["xl"], me["core"]
    sib = (me["s"], 2 * xl + 1 - core)
    xlo = (me["s"], 2 * (1 - xl) + core)
    yp, ym, y2, zp, zm, xo = (me[n] for n in ("yp", "ym", "y2", "zp", "zm", "xo"))
    met = hail([yp, ym, y2, zp, zm, xo, sib, xlo])

    def fetch(src, dst, index):
        copy = pltpu.make_async_copy(src, dst, local_sems.at[index])
        copy.start()
        return copy.wait

    get_k = fetch(k_ref, kk.at[0, 0], 0)
    get_v = fetch(v_ref, v_buf, 1)
    get_q = fetch(q_ref, q_buf, 2)
    get_g = fetch(g_ref, g_buf, 3)
    get_w = []
    for i, (a, b) in enumerate(((1 - xl, 1 - core), (1 - xl, core), (xl, 1 - core), (xl, core))):
        first = pl.multiple_of((2 * a + b) * ROWS, ROWS)
        get_w.append(fetch(w_ref.at[:, pl.ds(first, ROWS)], w_buf.at[i], 4 + i))
    get_lse = fetch(lse_ref, lse_buf, 8)
    get_par = fetch(par_ref, par_buf, 9)
    get_node = fetch(node_ref, node_buf, 10)
    get_o = fetch(o_ref, o_buf, 11)

    get_v()
    vt[0, 0] = v_buf[...].T
    get_k()
    get_q()
    for h in range(GRP):
        q4[0, :, pl.ds(h * BLK, BLK)] = q_buf[pl.ds(h * HD, HD), :]

    met()
    wires = Wires(send_sems, recv_sems)
    send = wires.send
    got = {}
    up, down = pl.ds(0, HALF), pl.ds(HALF, HALF)

    got["xk"] = send(kk.at[0, 0], kk.at[0, 1], xo)
    got["xv"] = send(vt.at[0, 0], vt.at[0, 1], xo)
    got["pk0"] = send(kk.at[0, 0], kk.at[1, 0], zp)
    got["mv0"] = send(vt.at[0, 0], vt.at[7, 0], zm)
    got["pv0"] = send(vt.at[0, 0], vt.at[1, 0], zp)
    got["mk0"] = send(kk.at[0, 0], kk.at[7, 0], zm)
    got["q1a"] = send(q4.at[0, up], q4.at[1, up], yp)
    got["q3b"] = send(q4.at[0, down], q4.at[3, down], ym)
    got["q1b"] = send(q4.at[0, down], q4.at[1, down], yp)
    got["q3a"] = send(q4.at[0, up], q4.at[3, up], ym)

    get_g()
    gt = g_buf[...].T

    def partial_sum(i):
        get_w[i]()
        return jnp.dot(gt, w_buf[i], preferred_element_type=F32)

    out_a[...] = partial_sum(0).astype(BF16)
    got["a"] = send(out_a, in_a, sib)
    part[...] = partial_sum(1)
    got["a"]()
    for c, (a, b) in enumerate(CUTS):
        cols = pl.ds(a * BLK, (b - a) * BLK)
        sum_b[:, cols] = (part[:, cols] + in_a[:, cols].astype(F32)).astype(BF16)
        got[f"b{c}"] = send(sum_b.at[:, cols], in_b.at[:, cols], xlo)
    out_c[...] = partial_sum(2).astype(BF16)
    got["c"] = send(out_c, in_c, sib)
    part[...] = partial_sum(3)

    def flip(d, e):
        kt[d, e] = kk[d, e].T

    def pass_on(name, buf, d, e, plus):
        got[name]()
        if plus:
            got[name] = send(buf.at[d, e], buf.at[d + 1, e], zp)
        else:
            got[name] = send(buf.at[NZ - d, e], buf.at[NZ - d - 1, e], zm)

    def pass_on_all(d, e):
        pass_on(f"pk{e}", kk, d, e, True)
        pass_on(f"mv{e}", vt, d, e, False)
        if d < 3 or e == 1 and d < 3:
            pass_on(f"pv{e}", vt, d, e, True)
            pass_on(f"mk{e}", kk, d, e, False)
        else:
            got[f"pv{e}"]()
            got[f"mk{e}"]()

    pass_on_all(1, 0)
    got["xk"]()
    got["pk1"] = send(kk.at[0, 1], kk.at[1, 1], zp)
    got["mk1"] = send(kk.at[0, 1], kk.at[7, 1], zm)
    got["xv"]()
    got["mv1"] = send(vt.at[0, 1], vt.at[7, 1], zm)
    got["pv1"] = send(vt.at[0, 1], vt.at[1, 1], zp)
    got["q1a"]()
    got["q2a"] = send(q4.at[1, up], q4.at[2, up], yp)
    got["q3b"]()
    got["q2b"] = send(q4.at[3, down], q4.at[2, down], ym)

    get_par()
    get_node()
    order, count = list_pairs(me, par_buf[...], node_buf[...])
    plan[0:1, 0:NODES] = order
    plan[1:2, :] = jnp.broadcast_to(count, (1, 128))

    for d, e in ((0, 0), (0, 1), (1, 0), (7, 0)):
        flip(d, e)
    get_o()
    get_lse()
    got["c"]()
    tail[0, 0:GRP, :] = lse_buf[...].astype(F32) * LOG2E

    def finish_grads(c):
        a, b = CUTS[c]
        got[f"b{c}"]()
        for h in range(a, b):
            cols = pl.ds(h * BLK, BLK)
            grad = part[:, cols] + in_c[:, cols].astype(F32) + in_b[:, cols].astype(F32)
            grad = grad.T.astype(BF16)
            g4[0, :, cols] = grad
            product = grad.astype(F32) * o_buf[pl.ds(h * HD, HD), :].astype(F32)
            tail[0, 8 + h : 9 + h, :] = jnp.sum(product, axis=0, keepdims=True)
        cols = pl.ds(a * BLK, (b - a) * BLK)
        got[f"g1{c}"] = send(g4.at[0, :, cols], g4.at[1, :, cols], yp)
        got[f"g3{c}"] = send(g4.at[0, :, cols], g4.at[3, :, cols], ym)
        return cols

    first = finish_grads(0)
    pass_on_all(2, 0)
    pass_on_all(1, 1)
    second = finish_grads(1)
    got["g21"] = send(g4.at[0, :, second], g4.at[2, :, second], y2)
    got["t1"] = send(tail.at[0], tail.at[1], yp)
    got["t3"] = send(tail.at[0], tail.at[3], ym)
    got["t2"] = send(tail.at[0], tail.at[2], y2)
    for d, e in ((1, 1), (7, 1), (2, 0), (6, 0)):
        flip(d, e)
    pass_on_all(3, 0)
    pass_on_all(2, 1)
    got["g10"]()
    got["g20"] = send(g4.at[1, :, first], g4.at[2, :, first], yp)
    for d, e in ((3, 0), (5, 0), (2, 1), (6, 1)):
        flip(d, e)
    pass_on_all(3, 1)
    for d, e in ((3, 1), (5, 1)):
        flip(d, e)
    got["pk0"]()
    flip(4, 0)
    got["pk1"]()
    flip(4, 1)
    for name in ("mv0", "mv1", "q1b", "q3a", "q2a", "q2b", "g30", "g11", "g31", "t1", "t3", "t2", "g21", "g20"):
        got[name]()
    wires.finish()


def gather(q, k, v, o, lse, g, w, par, node):
    blocks = (NZ, NX, HD, BLK)
    return pl.pallas_call(
        gather_kernel,
        out_shape=(
            pltpu.VMEM((NY, HD, ROWS), BF16),
            pltpu.VMEM((NY, HD, ROWS), BF16),
            pltpu.VMEM((NY, 16, BLK), F32),
            pltpu.VMEM(blocks, BF16),
            pltpu.VMEM(blocks, BF16),
            pltpu.VMEM(blocks, BF16),
            pltpu.VMEM((8, 128), jnp.int32),
        ),
        in_specs=[HBM] * 9,
        out_specs=(VMEM,) * 7,
        scratch_shapes=[
            pltpu.VMEM(g.shape, BF16),
            pltpu.VMEM((4, w.shape[0], ROWS), BF16),
            pltpu.VMEM((ROWS, BLK), BF16),
            pltpu.VMEM((GRP, BLK), BF16),
            pltpu.VMEM((ROWS, BLK), BF16),
            pltpu.VMEM((HD, BLK), BF16),
            pltpu.VMEM((1, NODES), jnp.int32),
            pltpu.VMEM((1, NODES), jnp.int32),
            pltpu.VMEM((BLK, ROWS), F32),
        ]
        + [pltpu.VMEM((BLK, ROWS), BF16)] * 6
        + [
            pltpu.SemaphoreType.DMA((12,)),
            pltpu.SemaphoreType.DMA((56,)),
            pltpu.SemaphoreType.DMA((56,)),
        ],
        compiler_params=pltpu.CompilerParams(
            collective_id=0, has_side_effects=True, vmem_limit_bytes=32 << 20
        ),
        name="gather_and_head_grads",
    )(*place(pltpu.HBM, q, k, v, o, lse, g, w, par, node))


def attend_kernel(plan, q4, g4, tail, kk, kt, vt, dq, dkv):
    def pair(qi, i, mask):
        zi, xi = i % NZ, i // NZ
        q_c, g_c = q4[qi], g4[qi]
        s_all = jnp.dot(kt[zi, xi], q_c, preferred_element_type=F32)
        dp_all = jnp.dot(vt[zi, xi], g_c, preferred_element_type=F32)
        w_parts, ds_parts = [], []
        for h in range(GRP):
            cols = slice(h * BLK, (h + 1) * BLK)
            p = jnp.exp2(s_all[:, cols] * (SCALE * LOG2E) - tail[qi, h : h + 1, :])
            if mask is not None:
                p = jnp.where(mask, p, 0.0)
            w_parts.append(p.astype(BF16))
            ds_parts.append((p * (dp_all[:, cols] - tail[qi, 8 + h : 9 + h, :])).astype(BF16))
        w_all = jnp.concatenate(w_parts, axis=1)
        ds_all = jnp.concatenate(ds_parts, axis=1)
        return (
            jnp.dot(kk[zi, xi], ds_all, preferred_element_type=F32),
            lax.dot_general(q_c, ds_all, NT, preferred_element_type=F32),
            lax.dot_general(g_c, w_all, NT, preferred_element_type=F32),
        )

    dq[pl.ds(1, NY - 1)] = jnp.zeros((NY - 1, HD, ROWS), F32)
    dkv[...] = jnp.zeros_like(dkv)
    key = lax.broadcasted_iota(jnp.int32, (BLK, BLK), 0)
    query = lax.broadcasted_iota(jnp.int32, (BLK, BLK), 1)
    dq[0], dkv[0, 0, 0], dkv[0, 0, 1] = pair(0, 0, key <= query)

    def one(t, carry):
        at = plan[0, t]
        qi, i = at // KEYS, at % KEYS
        zi, xi = i % NZ, i // NZ
        dq_t, dk_t, dv_t = pair(qi, i, None)
        dq[qi] += dq_t
        dkv[zi, xi, 0] += dk_t
        dkv[zi, xi, 1] += dv_t
        return carry

    lax.fori_loop(0, plan[1, 0], one, 0)


def attend(plan, q4, g4, tail, kk, kt, vt):
    return pl.pallas_call(
        attend_kernel,
        out_shape=(
            pltpu.VMEM((NY, HD, ROWS), F32),
            pltpu.VMEM((NZ, NX, 2, HD, BLK), F32),
        ),
        in_specs=[SMEM] + [VMEM] * 6,
        out_specs=(VMEM,) * 2,
        compiler_params=pltpu.CompilerParams(vmem_limit_bytes=32 << 20),
        name="attend_visible_pairs",
    )(plan, *place(pltpu.VMEM, q4, g4, tail, kk, kt, vt))


def scatter_kernel(
    dq, dkv, qp_in, qm_in, own, x_in,
    p_out, m_out, p_in, m_in, qp_out, qm_out, q2p_out, q2m_out, qp_half, qm_half, x_out,
    send_sems, recv_sems,
):
    me = where_am_i()
    yp, ym, zp, zm, xo = (me[n] for n in ("yp", "ym", "zp", "zm", "xo"))
    met = hail([yp, ym, zp, zm, xo])
    wires = Wires(send_sems, recv_sems)
    send = wires.send
    got = {}
    up, down = pl.ds(0, HALF), pl.ds(HALF, HALF)
    chunks = ((1, 0, True), (1, 1, False), (1, 1, True), (1, 0, False))
    chunks += tuple((0, kv, plus) for _, kv, plus in chunks)

    def stage(left, e, kv, plus):
        slot = NZ - left if plus else left
        out, land = (p_out, p_in) if plus else (m_out, m_in)
        long = plus == (kv == 0)
        value = dkv[slot, e, kv]
        if left < (4 if long else 3):
            got[e, kv, plus]()
            value = value + land[left, e, kv].astype(F32)
        out[left - 1, e, kv] = value.astype(BF16)
        got[e, kv, plus] = send(
            out.at[left - 1, e, kv], land.at[left - 1, e, kv], zp if plus else zm
        )

    q2p_out[...] = dq[2, up].astype(BF16)
    q2m_out[...] = dq[2, down].astype(BF16)
    qp_out[down, :] = dq[3, down].astype(BF16)
    qm_out[up, :] = dq[1, up].astype(BF16)
    met()
    for e, kv, plus in chunks:
        if plus == (kv == 0):
            stage(4, e, kv, plus)
    got["q2p"] = send(q2p_out, qp_half, yp)
    got["q2m"] = send(q2m_out, qm_half, ym)
    for e, kv, plus in chunks:
        if plus != (kv == 0):
            stage(3, e, kv, plus)
    got["qpd"] = send(qp_out.at[down], qp_in.at[down], yp)
    got["qmu"] = send(qm_out.at[up], qm_in.at[up], ym)

    def turn(left):
        for e in (1, 0):
            for e2, kv, plus in chunks:
                if e2 == e:
                    long = plus == (kv == 0)
                    if long:
                        stage(left, e, kv, plus)
                    elif left > 1:
                        stage(left - 1, e, kv, plus)

    turn(3)
    got["q2p"]()
    qp_out[up, :] = (dq[3, up] + qp_half[...].astype(F32)).astype(BF16)
    got["qpu"] = send(qp_out.at[up], qp_in.at[up], yp)
    got["q2m"]()
    qm_out[down, :] = (dq[1, down] + qm_half[...].astype(F32)).astype(BF16)
    got["qmd"] = send(qm_out.at[down], qm_in.at[down], ym)
    turn(2)
    turn(1)

    def total(e, kv):
        got[e, kv, True]()
        got[e, kv, False]()
        return dkv[0, e, kv] + p_in[0, e, kv].astype(F32) + m_in[0, e, kv].astype(F32)

    for kv in (0, 1):
        x_out[kv] = total(1, kv).astype(BF16)
        got["x", kv] = send(x_out.at[kv], x_in.at[kv], xo)
    for kv in (0, 1):
        own[kv] = total(0, kv)
    for name in ("qpd", "qmu", "qpu", "qmd", ("x", 0), ("x", 1)):
        got[name]()
    wires.finish()


def scatter(dq, dkv):
    ring = (4, NX, 2, HD, BLK)
    wide, half, pair = (HD, ROWS), (HALF, ROWS), (2, HD, BLK)
    return pl.pallas_call(
        scatter_kernel,
        out_shape=(
            pltpu.VMEM(wide, BF16),
            pltpu.VMEM(wide, BF16),
            pltpu.VMEM(pair, F32),
            pltpu.VMEM(pair, BF16),
        ),
        in_specs=[VMEM] * 2,
        out_specs=(VMEM,) * 4,
        scratch_shapes=[pltpu.VMEM(ring, BF16)] * 4
        + [pltpu.VMEM(wide, BF16)] * 2
        + [pltpu.VMEM(half, BF16)] * 4
        + [
            pltpu.VMEM(pair, BF16),
            pltpu.SemaphoreType.DMA((40,)),
            pltpu.SemaphoreType.DMA((40,)),
        ],
        compiler_params=pltpu.CompilerParams(
            collective_id=1, has_side_effects=True, vmem_limit_bytes=32 << 20
        ),
        name="scatter_sums",
    )(*place(pltpu.VMEM, dq, dkv))


def write_kernel(dq, qp_in, qm_in, own, x_in, q_out, k_out, v_out, q_buf, kv_buf, sems):
    copies = []
    for kv, (out, scale) in enumerate(((k_out, SCALE), (v_out, 1.0))):
        kv_buf[kv] = (own[kv] + x_in[kv].astype(F32)) * scale
        copies.append(pltpu.make_async_copy(kv_buf.at[kv], out, sems.at[kv]))
        copies[-1].start()
    for h in range(GRP):
        cols = pl.ds(h * BLK, BLK)
        total = dq[0, :, cols] + qp_in[:, cols].astype(F32) + qm_in[:, cols].astype(F32)
        q_buf[pl.ds(h * HD, HD), :] = total * SCALE
    copies.append(pltpu.make_async_copy(q_buf, q_out, sems.at[2]))
    copies[-1].start()
    for copy in copies:
        copy.wait()


def write(dq, qp_in, qm_in, own, x_in):
    return pl.pallas_call(
        write_kernel,
        out_shape=(
            jax.ShapeDtypeStruct((ROWS, BLK), F32),
            jax.ShapeDtypeStruct((HD, BLK), F32),
            jax.ShapeDtypeStruct((HD, BLK), F32),
        ),
        in_specs=[VMEM] * 5,
        out_specs=(HBM,) * 3,
        scratch_shapes=[
            pltpu.VMEM((ROWS, BLK), F32),
            pltpu.VMEM((2, HD, BLK), F32),
            pltpu.SemaphoreType.DMA((3,)),
        ],
        name="write_gradients",
    )(*place(pltpu.VMEM, dq, qp_in, qm_in, own, x_in))


def body(q, k, v, o, lse, g, w, parents, node_of):
    *rest, plan = gather(q, k, v, o, lse, g, w, parents[None, :], node_of[None, :])
    dq, dkv = attend(plan, *rest)
    return write(dq, *scatter(dq, dkv))


def solution(mesh):
    both, one = P("fsdp", "seq"), P()
    return jax.shard_map(
        body,
        mesh=mesh,
        in_specs=(both,) * 6 + (P("fsdp", None), one, one),
        out_specs=(both,) * 3,
        check_vma=False,
    )
```

```python
import math

import jax
import jax.numpy as jnp
from jax import lax
from jax.experimental import pallas as pl
from jax.experimental.pallas import tpu as pltpu
from jax.sharding import PartitionSpec as P

MESH = pl.DeviceIdType.MESH
HD = 128
BLK = 128
GRP = 5
ROWS = GRP * HD
NX, NZ, NY = 2, 8, 4
NODES = NX * NZ * NY
KEYS = NX * NZ
HALF = HD // 2
CUTS = ((0, 2), (2, GRP))
SCALE = HD**-0.5
LOG2E = math.log2(math.e)
F32, BF16 = jnp.float32, jnp.bfloat16
HBM = pl.BlockSpec(memory_space=pltpu.HBM)
VMEM = pl.BlockSpec(memory_space=pltpu.VMEM)
SMEM = pl.BlockSpec(memory_space=pltpu.SMEM)
NT = (((1,), (1,)), ((), ()))


def place(space, *arrays):
    return [pltpu.with_memory_space_constraint(array, space) for array in arrays]


def where_am_i():
    s, f = lax.axis_index("seq"), lax.axis_index("fsdp")
    xh, z, y = s // (NZ * NY), (s // NY) % NZ, s % NY
    at = lambda xh, z, y: (xh * NZ + z) * NY + y
    return dict(
        s=s,
        f=f,
        xl=f // 2,
        core=f % 2,
        xh=xh,
        z=z,
        y=y,
        yp=(at(xh, z, (y + 1) % NY), f),
        ym=(at(xh, z, (y + NY - 1) % NY), f),
        y2=(at(xh, z, (y + 2) % NY), f),
        zp=(at(xh, (z + 1) % NZ, y), f),
        zm=(at(xh, (z + NZ - 1) % NZ, y), f),
        xo=(at(1 - xh, z, y), f),
        xp=(at(1 - xh, (z + 1) % NZ, y), f),
        xm=(at(1 - xh, (z + NZ - 1) % NZ, y), f),
    )


def hail(partners):
    barrier = pltpu.get_barrier_semaphore()
    for partner in partners:
        pl.semaphore_signal(barrier, inc=1, device_id=partner, device_id_type=MESH)
    return lambda: pl.semaphore_wait(barrier, len(partners))


class Wires:
    def __init__(self, send_sems, recv_sems):
        self.send_sems, self.recv_sems, self.count, self.sent = send_sems, recv_sems, 0, []

    def send(self, src, dst, to):
        copy = pltpu.make_async_remote_copy(
            src_ref=src,
            dst_ref=dst,
            send_sem=self.send_sems.at[self.count],
            recv_sem=self.recv_sems.at[self.count],
            device_id=to,
            device_id_type=MESH,
        )
        self.count += 1
        copy.start()
        self.sent.append(copy)
        return copy.wait_recv

    def finish(self):
        for copy in self.sent:
            copy.wait_send()


def list_pairs(me, parents, node_of):
    iota = lambda dim: lax.broadcasted_iota(jnp.int32, (NODES, NODES), dim)
    hot = lambda mask: jnp.where(mask, 1.0, 0.0)
    dot = lambda a, b: jnp.dot(a, b, preferred_element_type=F32)
    rows, cols = iota(0), iota(1)
    reach = hot((rows == parents) | (rows == cols))
    for _ in range(NODES.bit_length()):
        reach = hot(dot(reach, reach) > 0.5)
    placed = hot(rows == node_of)
    k, q = cols % KEYS, cols // KEYS
    k_xh = jnp.where(k % NX > 0, 1 - me["xh"], me["xh"])
    k_z = (me["z"] + NZ - k // NX) % NZ
    q_y = (me["y"] + NY - q) % NY
    node_k = dot(placed, hot(rows == (k_xh * NZ + k_z) * NY + me["y"]))
    node_q = dot(placed, hot(rows == (me["xh"] * NZ + me["z"]) * NY + q_y))
    seen = hot(jnp.sum(node_k * dot(reach, node_q), axis=0, keepdims=True) > 0.5)
    before = dot(seen, hot((rows < cols) & (rows // KEYS == q)))
    pair = lax.broadcasted_iota(jnp.int32, (1, NODES), 1)
    place = (pair // KEYS * KEYS).astype(F32) + before
    spot = hot((rows.astype(F32) == place) & (seen > 0.5))
    from_end = (pair % KEYS - KEYS).astype(F32)
    order = lax.dot_general(from_end, spot, NT, preferred_element_type=F32) + KEYS
    counts = dot(seen, hot(rows // KEYS == cols))
    return order.astype(jnp.int32), counts.astype(jnp.int32)


def gather_kernel(
    q_ref, k_ref, v_ref, o_ref, lse_ref, g_ref, w_ref, par_ref, node_ref,
    q4, g4, tail, kk, kt, vt, plan,
    g_buf, w_buf, o_buf, lse_buf, q_buf, v_buf, par_buf, node_buf,
    part, out_a, in_a, sum_b, in_b, out_c, in_c,
    local_sems, send_sems, recv_sems,
):
    me = where_am_i()
    xl, core = me["xl"], me["core"]
    sib = (me["s"], 2 * xl + 1 - core)
    xlo = (me["s"], 2 * (1 - xl) + core)
    yp, ym, y2, zp, zm, xo, xp, xm = (me[n] for n in ("yp", "ym", "y2", "zp", "zm", "xo", "xp", "xm"))
    met = hail([yp, ym, y2, zp, zm, xo, xp, xm, sib, xlo])

    def fetch(src, dst, index):
        copy = pltpu.make_async_copy(src, dst, local_sems.at[index])
        copy.start()
        return copy.wait

    get_k = fetch(k_ref, kk.at[0, 0], 0)
    get_v = fetch(v_ref, v_buf, 1)
    get_q = fetch(q_ref, q_buf, 2)
    get_g = fetch(g_ref, g_buf, 3)
    get_w = []
    for i, (a, b) in enumerate(((1 - xl, 1 - core), (1 - xl, core), (xl, 1 - core), (xl, core))):
        first = pl.multiple_of((2 * a + b) * ROWS, ROWS)
        get_w.append(fetch(w_ref.at[:, pl.ds(first, ROWS)], w_buf.at[i], 4 + i))
    get_lse = fetch(lse_ref, lse_buf, 8)
    get_par = fetch(par_ref, par_buf, 9)
    get_node = fetch(node_ref, node_buf, 10)
    get_o = fetch(o_ref, o_buf, 11)

    get_v()
    vt[0, 0] = v_buf[...].T
    get_k()
    get_q()
    for h in range(GRP):
        q4[0, :, pl.ds(h * BLK, BLK)] = q_buf[pl.ds(h * HD, HD), :]

    met()
    wires = Wires(send_sems, recv_sems)
    send = wires.send
    got = {}
    up, down = pl.ds(0, HALF), pl.ds(HALF, HALF)

    got["pk1"] = send(kk.at[0, 0], kk.at[1, 1], xp)
    got["mv1"] = send(vt.at[0, 0], vt.at[7, 1], xm)
    got["pk0"] = send(kk.at[0, 0], kk.at[1, 0], zp)
    got["mv0"] = send(vt.at[0, 0], vt.at[7, 0], zm)
    got["pv1"] = send(vt.at[0, 0], vt.at[1, 1], xp)
    got["mk1"] = send(kk.at[0, 0], kk.at[7, 1], xm)
    got["pv0"] = send(vt.at[0, 0], vt.at[1, 0], zp)
    got["mk0"] = send(kk.at[0, 0], kk.at[7, 0], zm)
    got["q1a"] = send(q4.at[0, up], q4.at[1, up], yp)
    got["q3b"] = send(q4.at[0, down], q4.at[3, down], ym)
    got["q1b"] = send(q4.at[0, down], q4.at[1, down], yp)
    got["q3a"] = send(q4.at[0, up], q4.at[3, up], ym)
    got["xk"] = send(kk.at[0, 0], kk.at[0, 1], xo)
    got["xv"] = send(vt.at[0, 0], vt.at[0, 1], xo)

    get_g()
    gt = g_buf[...].T

    def partial_sum(i):
        get_w[i]()
        return jnp.dot(gt, w_buf[i], preferred_element_type=F32)

    out_a[...] = partial_sum(0).astype(BF16)
    got["a"] = send(out_a, in_a, sib)
    part[...] = partial_sum(1)
    got["a"]()
    for c, (a, b) in enumerate(CUTS):
        cols = pl.ds(a * BLK, (b - a) * BLK)
        sum_b[:, cols] = (part[:, cols] + in_a[:, cols].astype(F32)).astype(BF16)
        got[f"b{c}"] = send(sum_b.at[:, cols], in_b.at[:, cols], xlo)
    out_c[...] = partial_sum(2).astype(BF16)
    got["c"] = send(out_c, in_c, sib)
    part[...] = partial_sum(3)

    def flip(d, e):
        kt[d, e] = kk[d, e].T

    def pass_on(name, buf, d, e, plus):
        got[name]()
        if plus:
            got[name] = send(buf.at[d, e], buf.at[d + 1, e], zp)
        else:
            got[name] = send(buf.at[NZ - d, e], buf.at[NZ - d - 1, e], zm)

    def pass_on_all(d, e):
        pass_on(f"pk{e}", kk, d, e, True)
        pass_on(f"mv{e}", vt, d, e, False)
        if d < 3:
            pass_on(f"pv{e}", vt, d, e, True)
            pass_on(f"mk{e}", kk, d, e, False)
        else:
            got[f"pv{e}"]()
            got[f"mk{e}"]()

    pass_on_all(1, 0)
    pass_on_all(1, 1)
    got["q1a"]()
    got["q2a"] = send(q4.at[1, up], q4.at[2, up], yp)
    got["q3b"]()
    got["q2b"] = send(q4.at[3, down], q4.at[2, down], ym)

    get_par()
    get_node()
    order, counts = list_pairs(me, par_buf[...], node_buf[...])
    plan[0:1, 0:NODES] = order
    plan[1:2, 0:NODES] = counts
    for buf in (kk, kt, vt):
        buf[NZ, 0] = jnp.zeros((HD, BLK), BF16)

    got["xk"]()
    got["xv"]()
    for d, e in ((0, 0), (0, 1), (1, 0), (7, 0)):
        flip(d, e)
    get_o()
    get_lse()
    got["c"]()
    tail[0, 0:GRP, :] = lse_buf[...].astype(F32) * LOG2E

    def finish_grads(c):
        a, b = CUTS[c]
        got[f"b{c}"]()
        for h in range(a, b):
            cols = pl.ds(h * BLK, BLK)
            grad = part[:, cols] + in_c[:, cols].astype(F32) + in_b[:, cols].astype(F32)
            grad = grad.T.astype(BF16)
            g4[0, :, cols] = grad
            product = grad.astype(F32) * o_buf[pl.ds(h * HD, HD), :].astype(F32)
            tail[0, 8 + h : 9 + h, :] = jnp.sum(product, axis=0, keepdims=True)
        cols = pl.ds(a * BLK, (b - a) * BLK)
        got[f"g1{c}"] = send(g4.at[0, :, cols], g4.at[1, :, cols], yp)
        got[f"g3{c}"] = send(g4.at[0, :, cols], g4.at[3, :, cols], ym)
        return cols

    first = finish_grads(0)
    pass_on_all(2, 0)
    pass_on_all(2, 1)
    second = finish_grads(1)
    got["g21"] = send(g4.at[0, :, second], g4.at[2, :, second], y2)
    got["t1"] = send(tail.at[0], tail.at[1], yp)
    got["t3"] = send(tail.at[0], tail.at[3], ym)
    got["t2"] = send(tail.at[0], tail.at[2], y2)
    for d, e in ((1, 1), (7, 1), (2, 0), (6, 0)):
        flip(d, e)
    pass_on_all(3, 0)
    pass_on_all(3, 1)
    got["g10"]()
    got["g20"] = send(g4.at[1, :, first], g4.at[2, :, first], yp)
    for d, e in ((3, 0), (5, 0), (2, 1), (6, 1), (3, 1), (5, 1)):
        flip(d, e)
    got["pk0"]()
    flip(4, 0)
    got["pk1"]()
    flip(4, 1)
    for name in ("mv0", "mv1", "q1b", "q3a", "q2a", "q2b", "g30", "g11", "g31", "t1", "t3", "t2", "g21", "g20"):
        got[name]()
    wires.finish()


def gather(q, k, v, o, lse, g, w, par, node):
    blocks = (NZ + 1, NX, HD, BLK)
    return pl.pallas_call(
        gather_kernel,
        out_shape=(
            pltpu.VMEM((NY, HD, ROWS), BF16),
            pltpu.VMEM((NY, HD, ROWS), BF16),
            pltpu.VMEM((NY, 16, BLK), F32),
            pltpu.VMEM(blocks, BF16),
            pltpu.VMEM(blocks, BF16),
            pltpu.VMEM(blocks, BF16),
            pltpu.VMEM((8, 128), jnp.int32),
        ),
        in_specs=[HBM] * 9,
        out_specs=(VMEM,) * 7,
        scratch_shapes=[
            pltpu.VMEM(g.shape, BF16),
            pltpu.VMEM((4, w.shape[0], ROWS), BF16),
            pltpu.VMEM((ROWS, BLK), BF16),
            pltpu.VMEM((GRP, BLK), BF16),
            pltpu.VMEM((ROWS, BLK), BF16),
            pltpu.VMEM((HD, BLK), BF16),
            pltpu.VMEM((1, NODES), jnp.int32),
            pltpu.VMEM((1, NODES), jnp.int32),
            pltpu.VMEM((BLK, ROWS), F32),
        ]
        + [pltpu.VMEM((BLK, ROWS), BF16)] * 6
        + [
            pltpu.SemaphoreType.DMA((12,)),
            pltpu.SemaphoreType.DMA((56,)),
            pltpu.SemaphoreType.DMA((56,)),
        ],
        compiler_params=pltpu.CompilerParams(
            collective_id=0, has_side_effects=True, vmem_limit_bytes=32 << 20
        ),
        name="gather_and_head_grads",
    )(*place(pltpu.HBM, q, k, v, o, lse, g, w, par, node))


def attend_kernel(plan, q4, g4, tail, kk, kt, vt, dq, dkv):
    ahead = lax.broadcasted_iota(jnp.int32, (BLK, BLK), 0) - lax.broadcasted_iota(
        jnp.int32, (BLK, BLK), 1
    )

    def some(qi, first, count):
        at = [plan[0, qi * KEYS + first + u] for u in range(count)]
        at = [(i // NX, i % NX) for i in at]
        reach = jnp.where((qi == 0) & (first == 0), 0, BLK)
        join = lambda parts, dim: parts[0] if len(parts) == 1 else jnp.concatenate(parts, axis=dim)
        q_c, g_c = q4[qi], g4[qi]
        s_all = jnp.dot(join([kt[i] for i in at], 0), q_c, preferred_element_type=F32)
        dp_all = jnp.dot(join([vt[i] for i in at], 0), g_c, preferred_element_type=F32)
        w_parts, ds_parts = [], []
        for h in range(GRP):
            cols = slice(h * BLK, (h + 1) * BLK)
            p = jnp.exp2(s_all[:, cols] * (SCALE * LOG2E) - tail[qi, h : h + 1, :])
            head = jnp.where(ahead <= reach, p[:BLK], 0.0)
            p = head if count == 1 else jnp.concatenate([head, p[BLK:]], axis=0)
            w_parts.append(p.astype(BF16))
            ds_parts.append((p * (dp_all[:, cols] - tail[qi, 8 + h : 9 + h, :])).astype(BF16))
        w_all, ds_all = join(w_parts, 1), join(ds_parts, 1)
        dq[qi] += jnp.dot(join([kk[i] for i in at], 1), ds_all, preferred_element_type=F32)
        dk_t = lax.dot_general(q_c, ds_all, NT, preferred_element_type=F32)
        dv_t = lax.dot_general(g_c, w_all, NT, preferred_element_type=F32)
        for u, (zi, xi) in enumerate(at):
            dkv[zi, xi, 0] += dk_t[:, u * BLK : (u + 1) * BLK]
            dkv[zi, xi, 1] += dv_t[:, u * BLK : (u + 1) * BLK]

    dq[...] = jnp.zeros_like(dq)
    dkv[...] = jnp.zeros_like(dkv)

    def query_block(qi, carry):
        count = plan[1, qi]
        fours = (count + 1) // 4
        left = count - 4 * fours

        def four(t, carry):
            some(qi, 4 * t, 4)
            return carry

        lax.fori_loop(0, fours, four, 0)

        @pl.when(left == 2)
        def _():
            some(qi, 4 * fours, 2)

        @pl.when(left == 1)
        def _():
            some(qi, 4 * fours, 1)

        return carry

    lax.fori_loop(0, NY, query_block, 0)


def attend(plan, q4, g4, tail, kk, kt, vt):
    return pl.pallas_call(
        attend_kernel,
        out_shape=(
            pltpu.VMEM((NY, HD, ROWS), F32),
            pltpu.VMEM((NZ + 1, NX, 2, HD, BLK), F32),
        ),
        in_specs=[SMEM] + [VMEM] * 6,
        out_specs=(VMEM,) * 2,
        compiler_params=pltpu.CompilerParams(vmem_limit_bytes=32 << 20),
        name="attend_visible_pairs",
    )(plan, *place(pltpu.VMEM, q4, g4, tail, kk, kt, vt))


def scatter_kernel(
    dq, dkv, qp_in, qm_in, own,
    p_out, m_out, p_in, m_in, qp_out, qm_out, q2p_out, q2m_out, qp_half, qm_half, x_out, x_in,
    send_sems, recv_sems,
):
    me = where_am_i()
    yp, ym, zp, zm, xo, xp, xm = (me[n] for n in ("yp", "ym", "zp", "zm", "xo", "xp", "xm"))
    met = hail([yp, ym, zp, zm, xo, xp, xm])
    wires = Wires(send_sems, recv_sems)
    send = wires.send
    got = {}
    up, down = pl.ds(0, HALF), pl.ds(HALF, HALF)
    chunks = ((1, 0, True), (1, 1, False), (1, 1, True), (1, 0, False))
    chunks += tuple((0, kv, plus) for _, kv, plus in chunks)

    def stage(left, e, kv, plus):
        slot = NZ - left if plus else left
        out, land = (p_out, p_in) if plus else (m_out, m_in)
        long = plus == (kv == 0)
        value = dkv[slot, e, kv]
        if left < (4 if long else 3):
            got[e, kv, plus]()
            value = value + land[left, e, kv].astype(F32)
        out[left - 1, e, kv] = value.astype(BF16)
        if left == 1 and e == 1:
            land, to = x_in.at[plus + 1, kv], xp if plus else xm
        else:
            land, to = land.at[left - 1, e, kv], zp if plus else zm
        got[e, kv, plus] = send(out.at[left - 1, e, kv], land, to)

    q2p_out[...] = dq[2, up].astype(BF16)
    q2m_out[...] = dq[2, down].astype(BF16)
    qp_out[down, :] = dq[3, down].astype(BF16)
    qm_out[up, :] = dq[1, up].astype(BF16)
    met()
    for e, kv, plus in chunks:
        if plus == (kv == 0):
            stage(4, e, kv, plus)
    got["q2p"] = send(q2p_out, qp_half, yp)
    got["q2m"] = send(q2m_out, qm_half, ym)
    for e, kv, plus in chunks:
        if plus != (kv == 0):
            stage(3, e, kv, plus)
    got["qpd"] = send(qp_out.at[down], qp_in.at[down], yp)
    got["qmu"] = send(qm_out.at[up], qm_in.at[up], ym)
    x_out[...] = dkv[0, 1].astype(BF16)
    got["x"] = send(x_out, x_in.at[0], xo)

    def turn(left):
        for e in (1, 0):
            for e2, kv, plus in chunks:
                if e2 == e:
                    long = plus == (kv == 0)
                    if long:
                        stage(left, e, kv, plus)
                    elif left > 1:
                        stage(left - 1, e, kv, plus)

    turn(3)
    got["q2p"]()
    qp_out[up, :] = (dq[3, up] + qp_half[...].astype(F32)).astype(BF16)
    got["qpu"] = send(qp_out.at[up], qp_in.at[up], yp)
    got["q2m"]()
    qm_out[down, :] = (dq[1, down] + qm_half[...].astype(F32)).astype(BF16)
    got["qmd"] = send(qm_out.at[down], qm_in.at[down], ym)
    turn(2)
    turn(1)

    got["x"]()
    total = [dkv[0, 0, kv] + x_in[0, kv].astype(F32) for kv in (0, 1)]
    for e, kv, plus in sorted(chunks, key=lambda c: c[2] == (c[1] == 0)):
        got[e, kv, plus]()
        land = x_in.at[plus + 1, kv] if e == 1 else (p_in if plus else m_in).at[0, 0, kv]
        total[kv] = total[kv] + land[...].astype(F32)
    for kv in (0, 1):
        own[kv] = total[kv]
    for name in ("qpd", "qmu", "qpu", "qmd"):
        got[name]()
    wires.finish()


def scatter(dq, dkv):
    ring = (4, NX, 2, HD, BLK)
    wide, half, pair = (HD, ROWS), (HALF, ROWS), (2, HD, BLK)
    return pl.pallas_call(
        scatter_kernel,
        out_shape=(
            pltpu.VMEM(wide, BF16),
            pltpu.VMEM(wide, BF16),
            pltpu.VMEM(pair, F32),
        ),
        in_specs=[VMEM] * 2,
        out_specs=(VMEM,) * 3,
        scratch_shapes=[pltpu.VMEM(ring, BF16)] * 4
        + [pltpu.VMEM(wide, BF16)] * 2
        + [pltpu.VMEM(half, BF16)] * 4
        + [
            pltpu.VMEM(pair, BF16),
            pltpu.VMEM((3, *pair), BF16),
            pltpu.SemaphoreType.DMA((40,)),
            pltpu.SemaphoreType.DMA((40,)),
        ],
        compiler_params=pltpu.CompilerParams(
            collective_id=1, has_side_effects=True, vmem_limit_bytes=32 << 20
        ),
        name="scatter_sums",
    )(*place(pltpu.VMEM, dq, dkv))


def write_kernel(dq, qp_in, qm_in, own, q_out, k_out, v_out, q_buf, kv_buf, sems):
    copies = []
    for kv, (out, scale) in enumerate(((k_out, SCALE), (v_out, 1.0))):
        kv_buf[kv] = own[kv] * scale
        copies.append(pltpu.make_async_copy(kv_buf.at[kv], out, sems.at[kv]))
        copies[-1].start()
    for h in range(GRP):
        cols = pl.ds(h * BLK, BLK)
        total = dq[0, :, cols] + qp_in[:, cols].astype(F32) + qm_in[:, cols].astype(F32)
        q_buf[pl.ds(h * HD, HD), :] = total * SCALE
    copies.append(pltpu.make_async_copy(q_buf, q_out, sems.at[2]))
    copies[-1].start()
    for copy in copies:
        copy.wait()


def write(dq, qp_in, qm_in, own):
    return pl.pallas_call(
        write_kernel,
        out_shape=(
            jax.ShapeDtypeStruct((ROWS, BLK), F32),
            jax.ShapeDtypeStruct((HD, BLK), F32),
            jax.ShapeDtypeStruct((HD, BLK), F32),
        ),
        in_specs=[VMEM] * 4,
        out_specs=(HBM,) * 3,
        scratch_shapes=[
            pltpu.VMEM((ROWS, BLK), F32),
            pltpu.VMEM((2, HD, BLK), F32),
            pltpu.SemaphoreType.DMA((3,)),
        ],
        name="write_gradients",
    )(*place(pltpu.VMEM, dq, qp_in, qm_in, own))


def body(q, k, v, o, lse, g, w, parents, node_of):
    *rest, plan = gather(q, k, v, o, lse, g, w, parents[None, :], node_of[None, :])
    dq, dkv = attend(plan, *rest)
    return write(dq, *scatter(dq, dkv))


def solution(mesh):
    both, one = P("fsdp", "seq"), P()
    return jax.shard_map(
        body,
        mesh=mesh,
        in_specs=(both,) * 6 + (P("fsdp", None), one, one),
        out_specs=(both,) * 3,
        check_vma=False,
    )
```

```python
import math

import jax
import jax.numpy as jnp
from jax import lax
from jax.experimental import pallas as pl
from jax.experimental.pallas import tpu as pltpu
from jax.sharding import PartitionSpec as P

MESH = pl.DeviceIdType.MESH
HD = 128
BLK = 128
GRP = 5
ROWS = GRP * HD
NX, NZ, NY = 2, 8, 4
NODES = NX * NZ * NY
KEYS = NX * NZ
HALF = HD // 2
SCALE = HD**-0.5
LOG2E = math.log2(math.e)
UNIT = 4096
F32, BF16 = jnp.float32, jnp.bfloat16
HBM = pl.BlockSpec(memory_space=pltpu.HBM)
VMEM = pl.BlockSpec(memory_space=pltpu.VMEM)
SMEM = pl.BlockSpec(memory_space=pltpu.SMEM)
NT = (((1,), (1,)), ((), ()))


def place(space, *arrays):
    return [pltpu.with_memory_space_constraint(array, space) for array in arrays]


def where_am_i():
    s, f = lax.axis_index("seq"), lax.axis_index("fsdp")
    xh, z, y = s // (NZ * NY), (s // NY) % NZ, s % NY
    at = lambda xh, z, y: (xh * NZ + z) * NY + y
    return dict(
        s=s,
        f=f,
        xl=f // 2,
        core=f % 2,
        xh=xh,
        z=z,
        y=y,
        yp=(at(xh, z, (y + 1) % NY), f),
        ym=(at(xh, z, (y + NY - 1) % NY), f),
        y2=(at(xh, z, (y + 2) % NY), f),
        zp=(at(xh, (z + 1) % NZ, y), f),
        zm=(at(xh, (z + NZ - 1) % NZ, y), f),
        xo=(at(1 - xh, z, y), f),
        xp=(at(1 - xh, (z + 1) % NZ, y), f),
        xm=(at(1 - xh, (z + NZ - 1) % NZ, y), f),
    )


def hail(partners):
    barrier = pltpu.get_barrier_semaphore()
    for partner in partners:
        pl.semaphore_signal(barrier, inc=1, device_id=partner, device_id_type=MESH)
    return lambda: pl.semaphore_wait(barrier, len(partners))


class Wires:
    def __init__(self, send_sem, recv_sems, last_sem, unit):
        self.send_sem, self.recv_sems, self.last_sem, self.unit = send_sem, recv_sems, last_sem, unit
        self.count, self.sent, self.last = 0, 0, 0

    def send(self, src, dst, to, last=False):
        size = math.prod(src.shape) * src.dtype.itemsize // UNIT
        self.sent += size
        if last:
            self.last += size
            recv_sem = self.last_sem
        else:
            recv_sem = self.recv_sems.at[self.count]
            self.count += 1
        copy = pltpu.make_async_remote_copy(
            src_ref=src,
            dst_ref=dst,
            send_sem=self.send_sem,
            recv_sem=recv_sem,
            device_id=to,
            device_id_type=MESH,
        )
        copy.start()
        return None if last else copy.wait_recv

    def finish(self, to, sends=True):
        many = self.unit.at[pl.ds(0, self.sent if sends else self.last)]
        copy = pltpu.make_async_remote_copy(
            src_ref=many,
            dst_ref=many,
            send_sem=self.send_sem,
            recv_sem=self.last_sem,
            device_id=to,
            device_id_type=MESH,
        )
        if sends:
            copy.wait_send()
        else:
            copy.wait_recv()


def list_pairs(me, parents, node_of, plan):
    iota = lambda dim: lax.broadcasted_iota(jnp.int32, (NODES, NODES), dim)
    hot = lambda mask: jnp.where(mask, 1.0, 0.0).astype(BF16)
    dot = lambda a, b: jnp.dot(a, b, preferred_element_type=F32)
    rows, cols = iota(0), iota(1)
    reach = hot((rows == parents) | (rows == cols))
    for _ in range(NODES.bit_length()):
        reach = hot(dot(reach, reach) > 0.5)
        yield
    placed = hot(rows == node_of)
    k, q = cols % KEYS, cols // KEYS
    k_xh = jnp.where(k % NX > 0, 1 - me["xh"], me["xh"])
    k_z = (me["z"] + NZ - k // NX) % NZ
    q_y = (me["y"] + NY - q) % NY
    node_k = dot(placed, hot(rows == (k_xh * NZ + k_z) * NY + me["y"]))
    node_q = dot(placed, hot(rows == (me["xh"] * NZ + me["z"]) * NY + q_y))
    yield
    above = dot(reach, node_q.astype(BF16))
    seen = hot(jnp.sum(node_k * above, axis=0, keepdims=True) > 0.5)
    yield
    before = dot(seen, hot((rows < cols) & (rows // KEYS == q)))
    pair = lax.broadcasted_iota(jnp.int32, (1, NODES), 1)
    place = (pair // KEYS * KEYS).astype(F32) + before
    spot = hot((rows.astype(F32) == place) & (seen.astype(F32) > 0.5))
    from_end = (pair % KEYS - KEYS).astype(F32)
    order = lax.dot_general(from_end.astype(BF16), spot, NT, preferred_element_type=F32) + KEYS
    counts = dot(seen, hot(rows // KEYS == cols))
    plan[0:1, 0:NODES] = order.astype(jnp.int32)
    plan[1:2, 0:NODES] = counts.astype(jnp.int32)


def gather_kernel(
    q_ref, k_ref, v_ref, o_ref, lse_ref, g_ref, w_ref, par_ref, node_ref,
    q4, g4, tail, kk, kt, vt, plan,
    g_buf, w_buf, o_buf, lse_buf, q_buf, v_buf, par_buf, node_buf,
    part, out_a, in_a, sum_b, in_b, out_c, in_c,
    unit, local_sems, send_sem, recv_sems, last_sem,
):
    me = where_am_i()
    xl, core = me["xl"], me["core"]
    sib = (me["s"], 2 * xl + 1 - core)
    xlo = (me["s"], 2 * (1 - xl) + core)
    yp, ym, y2, zp, zm, xo, xp, xm = (me[n] for n in ("yp", "ym", "y2", "zp", "zm", "xo", "xp", "xm"))
    met = hail([yp, ym, y2, zp, zm, xo, xp, xm, sib, xlo])

    def fetch(src, dst, index):
        copy = pltpu.make_async_copy(src, dst, local_sems.at[index])
        copy.start()
        return copy.wait

    get_k = fetch(k_ref, kk.at[0, 0], 0)
    get_v = fetch(v_ref, v_buf, 1)
    get_g = fetch(g_ref, g_buf, 2)
    get_w = []
    for i, (a, b) in enumerate(((1 - xl, 1 - core), (1 - xl, core), (xl, 1 - core), (xl, core))):
        first = pl.multiple_of((2 * a + b) * ROWS, ROWS)
        get_w.append(fetch(w_ref.at[:, pl.ds(first, ROWS)], w_buf.at[i], 3 + i))
        if i == 0:
            get_q = fetch(q_ref, q_buf, 7)
    get_lse = fetch(lse_ref, lse_buf, 8)
    get_par = fetch(par_ref, par_buf, 9)
    get_node = fetch(node_ref, node_buf, 10)
    get_o = fetch(o_ref, o_buf, 11)

    got = {}
    up, down = pl.ds(0, HALF), pl.ds(HALF, HALF)
    wires = Wires(send_sem, recv_sems, last_sem, unit)
    send = wires.send

    get_v()
    vt[0, 0] = v_buf[...].T
    get_k()
    met()
    got["pk", 1] = send(kk.at[0, 0], kk.at[1, 1], xp)
    got["mv", 1] = send(vt.at[0, 0], vt.at[7, 1], xm)
    got["pk", 0] = send(kk.at[0, 0], kk.at[1, 0], zp)
    got["mv", 0] = send(vt.at[0, 0], vt.at[7, 0], zm)
    got["pv", 1] = send(vt.at[0, 0], vt.at[1, 1], xp)
    got["mk", 1] = send(kk.at[0, 0], kk.at[7, 1], xm)
    got["pv", 0] = send(vt.at[0, 0], vt.at[1, 0], zp)
    got["mk", 0] = send(kk.at[0, 0], kk.at[7, 0], zm)

    get_g()
    gt = g_buf[...].T

    def partial_sum(i):
        get_w[i]()
        return jnp.dot(gt, w_buf[i], preferred_element_type=F32)

    out_a[...] = partial_sum(0).astype(BF16)
    got["a"] = send(out_a, in_a, sib)
    get_q()
    for h in range(GRP):
        q4[0, :, pl.ds(h * BLK, BLK)] = q_buf[pl.ds(h * HD, HD), :]
    got["q1a"] = send(q4.at[0, up], q4.at[1, up], yp)
    got["q3b"] = send(q4.at[0, down], q4.at[3, down], ym)
    send(q4.at[0, down], q4.at[1, down], yp, last=True)
    send(q4.at[0, up], q4.at[3, up], ym, last=True)
    part[...] = partial_sum(1)
    got["a"]()
    for h in range(GRP):
        cols = pl.ds(h * BLK, BLK)
        sum_b[:, cols] = (part[:, cols] + in_a[:, cols].astype(F32)).astype(BF16)
        got["b", h] = send(sum_b.at[:, cols], in_b.at[:, cols], xlo)
    out_c[...] = partial_sum(2).astype(BF16)
    got["c"] = send(out_c, in_c, sib)
    send(kk.at[0, 0], kk.at[0, 1], xo, last=True)
    send(vt.at[0, 0], vt.at[0, 1], xo, last=True)
    part[...] = partial_sum(3)

    def pass_on(name, d, e):
        buf = kk if name[1] == "k" else vt
        last = d == 3 or d == 2 and name in ("pv", "mk")
        got[name, e]()
        if name[0] == "p":
            got[name, e] = send(buf.at[d, e], buf.at[d + 1, e], zp, last)
        else:
            got[name, e] = send(buf.at[NZ - d, e], buf.at[NZ - d - 1, e], zm, last)

    def finish_grad(h):
        cols = pl.ds(h * BLK, BLK)
        got["b", h]()
        grad = part[:, cols] + in_c[:, cols].astype(F32) + in_b[:, cols].astype(F32)
        grad = grad.T.astype(BF16)
        g4[0, :, cols] = grad
        got["g1", h] = send(g4.at[0, :, cols], g4.at[1, :, cols], yp, h in (2, 3))
        got["g3", h] = send(g4.at[0, :, cols], g4.at[3, :, cols], ym, h in (0, 1))
        product = grad.astype(F32) * o_buf[pl.ds(h * HD, HD), :].astype(F32)
        tail[0, 8 + h : 9 + h, :] = jnp.sum(product, axis=0, keepdims=True)

    def forward_grad(h, rows, plus):
        cols = pl.ds(h * BLK, BLK)
        slot, to = (1, yp) if plus else (3, ym)
        send(g4.at[slot, rows, cols], g4.at[2, rows, cols], to, last=True)

    every = pl.ds(0, HD)
    get_par()
    get_node()
    listing = list_pairs(me, par_buf[...], node_buf[...], plan)
    next(listing)
    for name in ("pk", "mv", "pv", "mk"):
        pass_on(name, 1, 0)
    get_lse()
    tail[0, 0:GRP, :] = lse_buf[...].astype(F32) * LOG2E
    get_o()
    got["c"]()
    for name in ("pk", "mv", "pv", "mk"):
        pass_on(name, 1, 1)
    next(listing)
    finish_grad(0)
    got["q1a"]()
    send(q4.at[1, up], q4.at[2, up], yp, last=True)
    got["q3b"]()
    send(q4.at[3, down], q4.at[2, down], ym, last=True)
    finish_grad(1)
    pass_on("pk", 2, 0)
    pass_on("mv", 2, 0)
    finish_grad(2)
    pass_on("pv", 2, 0)
    pass_on("mk", 2, 0)
    pass_on("pk", 2, 1)
    pass_on("mv", 2, 1)
    finish_grad(3)
    pass_on("pv", 2, 1)
    pass_on("mk", 2, 1)
    finish_grad(4)
    send(tail.at[0], tail.at[1], yp, last=True)
    send(tail.at[0], tail.at[3], ym, last=True)
    send(tail.at[0], tail.at[2], y2, last=True)
    got["g1", 0]()
    forward_grad(0, every, True)
    next(listing)
    got["g1", 1]()
    forward_grad(1, every, True)
    pass_on("pk", 3, 0)
    pass_on("mv", 3, 0)
    next(listing)
    got["g3", 2]()
    forward_grad(2, every, False)
    pass_on("pk", 3, 1)
    pass_on("mv", 3, 1)
    got["g3", 3]()
    forward_grad(3, every, False)
    got["g1", 4]()
    forward_grad(4, up, True)
    got["g3", 4]()
    forward_grad(4, down, False)
    for _ in listing:
        pass
    for buf in (kk, kt, vt):
        buf[NZ, 0] = jnp.zeros((HD, BLK), BF16)
    wires.finish(zp, sends=False)
    for d in range(NZ):
        for e in range(NX):
            kt[d, e] = kk[d, e].T
    wires.finish(zp)


def gather(q, k, v, o, lse, g, w, par, node):
    blocks = (NZ + 1, NX, HD, BLK)
    return pl.pallas_call(
        gather_kernel,
        out_shape=(
            pltpu.VMEM((NY, HD, ROWS), BF16),
            pltpu.VMEM((NY, HD, ROWS), BF16),
            pltpu.VMEM((NY, 16, BLK), F32),
            pltpu.VMEM(blocks, BF16),
            pltpu.VMEM(blocks, BF16),
            pltpu.VMEM(blocks, BF16),
            pltpu.VMEM((8, 128), jnp.int32),
        ),
        in_specs=[HBM] * 9,
        out_specs=(VMEM,) * 7,
        scratch_shapes=[
            pltpu.VMEM(g.shape, BF16),
            pltpu.VMEM((4, w.shape[0], ROWS), BF16),
            pltpu.VMEM((ROWS, BLK), BF16),
            pltpu.VMEM((GRP, BLK), BF16),
            pltpu.VMEM((ROWS, BLK), BF16),
            pltpu.VMEM((HD, BLK), BF16),
            pltpu.VMEM((1, NODES), jnp.int32),
            pltpu.VMEM((1, NODES), jnp.int32),
            pltpu.VMEM((BLK, ROWS), F32),
        ]
        + [pltpu.VMEM((BLK, ROWS), BF16)] * 6
        + [
            pltpu.VMEM((640, 16, 128), BF16),
            pltpu.SemaphoreType.DMA((12,)),
            pltpu.SemaphoreType.DMA(()),
            pltpu.SemaphoreType.DMA((36,)),
            pltpu.SemaphoreType.DMA(()),
        ],
        compiler_params=pltpu.CompilerParams(
            collective_id=0, has_side_effects=True, vmem_limit_bytes=32 << 20
        ),
        name="gather_and_head_grads",
    )(*place(pltpu.HBM, q, k, v, o, lse, g, w, par, node))


def attend_kernel(plan, q4, g4, tail, kk, kt, vt, dq, dkv):
    ahead = lax.broadcasted_iota(jnp.int32, (BLK, BLK), 0) - lax.broadcasted_iota(
        jnp.int32, (BLK, BLK), 1
    )

    def some(qi, first, count):
        at = [plan[0, qi * KEYS + first + u] for u in range(count)]
        at = [(i // NX, i % NX) for i in at]
        reach = jnp.where((qi == 0) & (first == 0), 0, BLK)
        join = lambda parts, dim: parts[0] if len(parts) == 1 else jnp.concatenate(parts, axis=dim)
        q_c, g_c = q4[qi], g4[qi]
        s_all = jnp.dot(join([kt[i] for i in at], 0), q_c, preferred_element_type=F32)
        dp_all = jnp.dot(join([vt[i] for i in at], 0), g_c, preferred_element_type=F32)
        w_parts, ds_parts = [], []
        for h in range(GRP):
            cols = slice(h * BLK, (h + 1) * BLK)
            p = jnp.exp2(s_all[:, cols] * (SCALE * LOG2E) - tail[qi, h : h + 1, :])
            head = jnp.where(ahead <= reach, p[:BLK], 0.0)
            p = head if count == 1 else jnp.concatenate([head, p[BLK:]], axis=0)
            w_parts.append(p.astype(BF16))
            ds_parts.append((p * (dp_all[:, cols] - tail[qi, 8 + h : 9 + h, :])).astype(BF16))
        w_all, ds_all = join(w_parts, 1), join(ds_parts, 1)
        dq[qi] += jnp.dot(join([kk[i] for i in at], 1), ds_all, preferred_element_type=F32)
        dk_t = lax.dot_general(q_c, ds_all, NT, preferred_element_type=F32)
        dv_t = lax.dot_general(g_c, w_all, NT, preferred_element_type=F32)
        for u, (zi, xi) in enumerate(at):
            dkv[zi, xi, 0] += dk_t[:, u * BLK : (u + 1) * BLK]
            dkv[zi, xi, 1] += dv_t[:, u * BLK : (u + 1) * BLK]

    dq[...] = jnp.zeros_like(dq)
    dkv[...] = jnp.zeros_like(dkv)

    def query_block(qi, carry):
        count = plan[1, qi]
        fours = (count + 1) // 4
        left = count - 4 * fours

        def four(t, carry):
            some(qi, 4 * t, 4)
            return carry

        lax.fori_loop(0, fours, four, 0)

        @pl.when(left == 2)
        def _():
            some(qi, 4 * fours, 2)

        @pl.when(left == 1)
        def _():
            some(qi, 4 * fours, 1)

        return carry

    lax.fori_loop(0, NY, query_block, 0)


def attend(plan, q4, g4, tail, kk, kt, vt):
    return pl.pallas_call(
        attend_kernel,
        out_shape=(
            pltpu.VMEM((NY, HD, ROWS), F32),
            pltpu.VMEM((NZ + 1, NX, 2, HD, BLK), F32),
        ),
        in_specs=[SMEM] + [VMEM] * 6,
        out_specs=(VMEM,) * 2,
        compiler_params=pltpu.CompilerParams(vmem_limit_bytes=32 << 20),
        name="attend_visible_pairs",
    )(plan, *place(pltpu.VMEM, q4, g4, tail, kk, kt, vt))


def scatter_kernel(
    dq, dkv, qp_in, qm_in, own,
    p_out, m_out, p_in, m_in, qp_out, qm_out, q2p_out, q2m_out, qp_half, qm_half, x_out, x_in,
    unit, send_sem, recv_sems, last_sem,
):
    me = where_am_i()
    yp, ym, zp, zm, xo, xp, xm = (me[n] for n in ("yp", "ym", "zp", "zm", "xo", "xp", "xm"))
    met = hail([yp, ym, zp, zm, xo, xp, xm])
    wires = Wires(send_sem, recv_sems, last_sem, unit)
    send = wires.send
    got = {}
    up, down = pl.ds(0, HALF), pl.ds(HALF, HALF)
    chunks = ((1, 0, True), (1, 1, False), (1, 1, True), (1, 0, False))
    chunks += tuple((0, kv, plus) for _, kv, plus in chunks)

    def stage(left, e, kv, plus):
        slot = NZ - left if plus else left
        out, land = (p_out, p_in) if plus else (m_out, m_in)
        long = plus == (kv == 0)
        value = dkv[slot, e, kv]
        if left < (4 if long else 3):
            got[e, kv, plus]()
            value = value + land[left, e, kv].astype(F32)
        if left == 1:
            if ("x", slot) in got:
                got.pop(("x", slot))()
            got[1, kv, plus]()
            value = value + x_in[1 - plus, kv].astype(F32) + land[1, 1, kv].astype(F32)
        out[left - 1, e, kv] = value.astype(BF16)
        to = (xp if plus else xm) if (left, e) == (2, 1) else (zp if plus else zm)
        got[e, kv, plus] = send(
            out.at[left - 1, e, kv], land.at[left - 1, e, kv], to, left == 1
        )

    q2p_out[...] = dq[2, up].astype(BF16)
    q2m_out[...] = dq[2, down].astype(BF16)
    qp_out[down, :] = dq[3, down].astype(BF16)
    qm_out[up, :] = dq[1, up].astype(BF16)
    met()
    for e, kv, plus in chunks:
        if plus == (kv == 0):
            stage(4, e, kv, plus)
    got["q2p"] = send(q2p_out, qp_half, yp)
    got["q2m"] = send(q2m_out, qm_half, ym)
    for e, kv, plus in chunks:
        if plus != (kv == 0):
            stage(3, e, kv, plus)
    send(qp_out.at[down], qp_in.at[down], yp, last=True)
    send(qm_out.at[up], qm_in.at[up], ym, last=True)
    for place, slot in enumerate((7, 1, 0)):
        x_out[place] = dkv[slot, 1].astype(BF16)
        got["x", slot] = send(x_out.at[place], x_in.at[place], xo, slot == 0)

    def turn(left):
        for e in (1, 0):
            for e2, kv, plus in chunks:
                step = left if plus == (kv == 0) else left - 1
                if e2 == e and step > e:
                    stage(step, e, kv, plus)

    turn(3)
    got["q2p"]()
    qp_out[up, :] = (dq[3, up] + qp_half[...].astype(F32)).astype(BF16)
    send(qp_out.at[up], qp_in.at[up], yp, last=True)
    got["q2m"]()
    qm_out[down, :] = (dq[1, down] + qm_half[...].astype(F32)).astype(BF16)
    send(qm_out.at[down], qm_in.at[down], ym, last=True)
    turn(2)
    turn(1)

    wires.finish(zp, sends=False)
    for kv in (0, 1):
        total = dkv[0, 0, kv] + x_in[2, kv].astype(F32)
        own[kv] = total + p_in[0, 0, kv].astype(F32) + m_in[0, 0, kv].astype(F32)
    wires.finish(zp)


def scatter(dq, dkv):
    ring = (4, NX, 2, HD, BLK)
    wide, half, pair = (HD, ROWS), (HALF, ROWS), (2, HD, BLK)
    return pl.pallas_call(
        scatter_kernel,
        out_shape=(
            pltpu.VMEM(wide, BF16),
            pltpu.VMEM(wide, BF16),
            pltpu.VMEM(pair, F32),
        ),
        in_specs=[VMEM] * 2,
        out_specs=(VMEM,) * 3,
        scratch_shapes=[pltpu.VMEM(ring, BF16)] * 4
        + [pltpu.VMEM(wide, BF16)] * 2
        + [pltpu.VMEM(half, BF16)] * 4
        + [
            pltpu.VMEM((3, *pair), BF16),
            pltpu.VMEM((3, *pair), BF16),
            pltpu.VMEM((400, 16, 128), BF16),
            pltpu.SemaphoreType.DMA(()),
            pltpu.SemaphoreType.DMA((24,)),
            pltpu.SemaphoreType.DMA(()),
        ],
        compiler_params=pltpu.CompilerParams(
            collective_id=1, has_side_effects=True, vmem_limit_bytes=32 << 20
        ),
        name="scatter_sums",
    )(*place(pltpu.VMEM, dq, dkv))


def write_kernel(dq, qp_in, qm_in, own, q_out, k_out, v_out, q_buf, kv_buf, sems):
    copies = []
    for kv, (out, scale) in enumerate(((k_out, SCALE), (v_out, 1.0))):
        kv_buf[kv] = own[kv] * scale
        copies.append(pltpu.make_async_copy(kv_buf.at[kv], out, sems.at[kv]))
        copies[-1].start()
    for h in range(GRP):
        cols = pl.ds(h * BLK, BLK)
        total = dq[0, :, cols] + qp_in[:, cols].astype(F32) + qm_in[:, cols].astype(F32)
        q_buf[pl.ds(h * HD, HD), :] = total * SCALE
    copies.append(pltpu.make_async_copy(q_buf, q_out, sems.at[2]))
    copies[-1].start()
    for copy in copies:
        copy.wait()


def write(dq, qp_in, qm_in, own):
    return pl.pallas_call(
        write_kernel,
        out_shape=(
            jax.ShapeDtypeStruct((ROWS, BLK), F32),
            jax.ShapeDtypeStruct((HD, BLK), F32),
            jax.ShapeDtypeStruct((HD, BLK), F32),
        ),
        in_specs=[VMEM] * 4,
        out_specs=(HBM,) * 3,
        scratch_shapes=[
            pltpu.VMEM((ROWS, BLK), F32),
            pltpu.VMEM((2, HD, BLK), F32),
            pltpu.SemaphoreType.DMA((3,)),
        ],
        name="write_gradients",
    )(*place(pltpu.VMEM, dq, qp_in, qm_in, own))


def body(q, k, v, o, lse, g, w, parents, node_of):
    *rest, plan = gather(q, k, v, o, lse, g, w, parents[None, :], node_of[None, :])
    dq, dkv = attend(plan, *rest)
    return write(dq, *scatter(dq, dkv))


def solution(mesh):
    both, one = P("fsdp", "seq"), P()
    return jax.shard_map(
        body,
        mesh=mesh,
        in_specs=(both,) * 6 + (P("fsdp", None), one, one),
        out_specs=(both,) * 3,
        check_vma=False,
    )
```

```python
import math

import jax
import jax.numpy as jnp
from jax import lax
from jax.experimental import pallas as pl
from jax.experimental.pallas import tpu as pltpu
from jax.sharding import PartitionSpec as P

MESH = pl.DeviceIdType.MESH
HD = 128
BLK = 128
GRP = 5
ROWS = GRP * HD
NX, NZ, NY = 2, 8, 4
NODES = NX * NZ * NY
KEYS = NX * NZ
HALF = HD // 2
SCALE = HD**-0.5
LOG2E = math.log2(math.e)
UNIT = 4096
F32, BF16 = jnp.float32, jnp.bfloat16
HBM = pl.BlockSpec(memory_space=pltpu.HBM)
VMEM = pl.BlockSpec(memory_space=pltpu.VMEM)
SMEM = pl.BlockSpec(memory_space=pltpu.SMEM)
NT = (((1,), (1,)), ((), ()))


def place(space, *arrays):
    return [pltpu.with_memory_space_constraint(array, space) for array in arrays]


def where_am_i():
    s, f = lax.axis_index("seq"), lax.axis_index("fsdp")
    xh, z, y = s // (NZ * NY), (s // NY) % NZ, s % NY
    at = lambda xh, z, y: (xh * NZ + z) * NY + y
    return dict(
        s=s,
        f=f,
        xl=f // 2,
        core=f % 2,
        xh=xh,
        z=z,
        y=y,
        yp=(at(xh, z, (y + 1) % NY), f),
        ym=(at(xh, z, (y + NY - 1) % NY), f),
        y2=(at(xh, z, (y + 2) % NY), f),
        zp=(at(xh, (z + 1) % NZ, y), f),
        zm=(at(xh, (z + NZ - 1) % NZ, y), f),
        zp2=(at(xh, (z + 2) % NZ, y), f),
        zm2=(at(xh, (z + NZ - 2) % NZ, y), f),
        xo=(at(1 - xh, z, y), f),
        xp=(at(1 - xh, (z + 1) % NZ, y), f),
        xm=(at(1 - xh, (z + NZ - 1) % NZ, y), f),
    )


def hail(partners):
    barrier = pltpu.get_barrier_semaphore()
    for partner in partners:
        pl.semaphore_signal(barrier, inc=1, device_id=partner, device_id_type=MESH)
    return lambda: pl.semaphore_wait(barrier, len(partners))


class Wires:
    def __init__(self, send_sem, recv_sems, last_sem, unit):
        self.send_sem, self.recv_sems, self.last_sem, self.unit = send_sem, recv_sems, last_sem, unit
        self.count, self.sent, self.last = 0, 0, 0

    def send(self, src, dst, to, last=False):
        size = math.prod(src.shape) * src.dtype.itemsize // UNIT
        self.sent += size
        if last:
            self.last += size
            recv_sem = self.last_sem
        else:
            recv_sem = self.recv_sems.at[self.count]
            self.count += 1
        copy = pltpu.make_async_remote_copy(
            src_ref=src,
            dst_ref=dst,
            send_sem=self.send_sem,
            recv_sem=recv_sem,
            device_id=to,
            device_id_type=MESH,
        )
        copy.start()
        return None if last else copy.wait_recv

    def finish(self, to, sends=True):
        many = self.unit.at[pl.ds(0, self.sent if sends else self.last)]
        copy = pltpu.make_async_remote_copy(
            src_ref=many,
            dst_ref=many,
            send_sem=self.send_sem,
            recv_sem=self.last_sem,
            device_id=to,
            device_id_type=MESH,
        )
        if sends:
            copy.wait_send()
        else:
            copy.wait_recv()


def vouch(other, sem):
    pl.semaphore_signal(sem, inc=1, device_id=other, device_id_type=MESH)


def list_pairs(me, parents, node_of, plan):
    iota = lambda dim: lax.broadcasted_iota(jnp.int32, (NODES, NODES), dim)
    hot = lambda mask: jnp.where(mask, 1.0, 0.0).astype(BF16)
    dot = lambda a, b: jnp.dot(a, b, preferred_element_type=F32)
    rows, cols = iota(0), iota(1)
    reach = hot((rows == parents) | (rows == cols))
    for _ in range(NODES.bit_length()):
        reach = hot(dot(reach, reach) > 0.5)
        yield
    placed = hot(rows == node_of)
    k, q = cols % KEYS, cols // KEYS
    k_xh = jnp.where(k % NX > 0, 1 - me["xh"], me["xh"])
    k_z = (me["z"] + NZ - k // NX) % NZ
    q_y = (me["y"] + NY - q) % NY
    node_k = dot(placed, hot(rows == (k_xh * NZ + k_z) * NY + me["y"]))
    node_q = dot(placed, hot(rows == (me["xh"] * NZ + me["z"]) * NY + q_y))
    yield
    above = dot(reach, node_q.astype(BF16))
    seen = hot(jnp.sum(node_k * above, axis=0, keepdims=True) > 0.5)
    yield
    before = dot(seen, hot((rows < cols) & (rows // KEYS == q)))
    pair = lax.broadcasted_iota(jnp.int32, (1, NODES), 1)
    place = (pair // KEYS * KEYS).astype(F32) + before
    spot = hot((rows.astype(F32) == place) & (seen.astype(F32) > 0.5))
    from_end = (pair % KEYS - KEYS).astype(F32)
    order = lax.dot_general(from_end.astype(BF16), spot, NT, preferred_element_type=F32) + KEYS
    counts = dot(seen, hot(rows // KEYS == cols))
    plan[0:1, 0:NODES] = order.astype(jnp.int32)
    plan[1:2, 0:NODES] = counts.astype(jnp.int32)


def gather_kernel(
    q_ref, k_ref, v_ref, o_ref, lse_ref, g_ref, w_ref, par_ref, node_ref,
    q4, g4, tail, kk, kt, vt, plan,
    g_buf, w_buf, o_buf, lse_buf, q_buf, v_buf, par_buf, node_buf,
    part, out_a, in_a, sum_b, in_b, out_c, in_c,
    unit, local_sems, send_sem, recv_sems, last_sem,
):
    me = where_am_i()
    xl, core = me["xl"], me["core"]
    sib = (me["s"], 2 * xl + 1 - core)
    xlo = (me["s"], 2 * (1 - xl) + core)
    near = [me[n] for n in ("yp", "ym", "y2", "zp", "zm", "zp2", "zm2", "xo")]
    yp, ym, y2, zp, zm, zp2, zm2, xo = near
    met = hail(near + [sib, xlo])

    def fetch(src, dst, index):
        copy = pltpu.make_async_copy(src, dst, local_sems.at[index])
        copy.start()
        return copy.wait

    get_k = fetch(k_ref, kk.at[0, 0], 0)
    get_v = fetch(v_ref, v_buf, 1)
    get_g = fetch(g_ref, g_buf, 2)
    get_w = []
    for i, (a, b) in enumerate(((1 - xl, 1 - core), (1 - xl, core), (xl, 1 - core), (xl, core))):
        first = pl.multiple_of((2 * a + b) * ROWS, ROWS)
        get_w.append(fetch(w_ref.at[:, pl.ds(first, ROWS)], w_buf.at[i], 3 + i))
        if i == 0:
            get_q = fetch(q_ref, q_buf, 7)
    get_lse = fetch(lse_ref, lse_buf, 8)
    get_par = fetch(par_ref, par_buf, 9)
    get_node = fetch(node_ref, node_buf, 10)
    get_o = fetch(o_ref, o_buf, 11)

    got = {}
    up, down = pl.ds(0, HALF), pl.ds(HALF, HALF)
    wires = Wires(send_sem, recv_sems, last_sem, unit)
    send = wires.send

    get_v()
    vt[0, 0] = v_buf[...].T
    get_k()
    get_q()
    for h in range(GRP):
        q4[0, :, pl.ds(h * BLK, BLK)] = q_buf[pl.ds(h * HD, HD), :]
    get_g()
    gt = g_buf[...].T

    def partial_sum(i):
        get_w[i]()
        return jnp.dot(gt, w_buf[i], preferred_element_type=F32)

    met()
    got["xk"] = send(kk.at[0, 0], kk.at[0, 1], xo)
    got["xv"] = send(vt.at[0, 0], vt.at[0, 1], xo)
    got["pk", 0] = send(kk.at[0, 0], kk.at[1, 0], zp)
    got["mv", 0] = send(vt.at[0, 0], vt.at[7, 0], zm)
    got["pv", 0] = send(vt.at[0, 0], vt.at[1, 0], zp)
    got["mk", 0] = send(kk.at[0, 0], kk.at[7, 0], zm)
    got["q1a"] = send(q4.at[0, up], q4.at[1, up], yp)
    got["q3b"] = send(q4.at[0, down], q4.at[3, down], ym)
    send(q4.at[0, down], q4.at[1, down], yp, last=True)
    send(q4.at[0, up], q4.at[3, up], ym, last=True)
    out_a[...] = partial_sum(0).astype(BF16)
    got["a"] = send(out_a, in_a, sib)
    part[...] = partial_sum(1)
    got["a"]()
    for h in range(GRP):
        cols = pl.ds(h * BLK, BLK)
        sum_b[:, cols] = (part[:, cols] + in_a[:, cols].astype(F32)).astype(BF16)
        got["b", h] = send(sum_b.at[:, cols], in_b.at[:, cols], xlo)
    out_c[...] = partial_sum(2).astype(BF16)
    got["c"] = send(out_c, in_c, sib)
    part[...] = partial_sum(3)

    def pass_on(name, d, e):
        buf = kk if name[1] == "k" else vt
        last = d == 3 or d == 2 and name in ("pv", "mk")
        got[name, e]()
        here, there, to = (d, d + 1, zp) if name[0] == "p" else (NZ - d, NZ - d - 1, zm)
        got[name, e] = send(buf.at[here, e], buf.at[there, e], to, last)

    def finish_grad(h):
        cols = pl.ds(h * BLK, BLK)
        got["b", h]()
        grad = part[:, cols] + in_c[:, cols].astype(F32) + in_b[:, cols].astype(F32)
        grad = grad.T.astype(BF16)
        g4[0, :, cols] = grad
        got["g1", h] = send(g4.at[0, :, cols], g4.at[1, :, cols], yp, h in (2, 3))
        got["g3", h] = send(g4.at[0, :, cols], g4.at[3, :, cols], ym, h in (0, 1))
        product = grad.astype(F32) * o_buf[pl.ds(h * HD, HD), :].astype(F32)
        tail[0, 8 + h : 9 + h, :] = jnp.sum(product, axis=0, keepdims=True)

    def forward_grad(h, rows, plus):
        cols = pl.ds(h * BLK, BLK)
        slot, to = (1, yp) if plus else (3, ym)
        send(g4.at[slot, rows, cols], g4.at[2, rows, cols], to, last=True)

    every = pl.ds(0, HD)
    get_par()
    get_node()
    get_lse()
    get_o()
    tail[0, 0:GRP, :] = lse_buf[...].astype(F32) * LOG2E
    got["c"]()
    for name in ("pk", "mv", "pv", "mk"):
        pass_on(name, 1, 0)
    got["xk"]()
    got["pk", 1] = send(kk.at[0, 1], kk.at[2, 1], zp2)
    got["mk", 1] = send(kk.at[0, 1], kk.at[6, 1], zm2)
    got["xv"]()
    got["mv", 1] = send(vt.at[0, 1], vt.at[6, 1], zm2)
    got["pv", 1] = send(vt.at[0, 1], vt.at[2, 1], zp2)
    finish_grad(0)
    finish_grad(1)
    finish_grad(2)
    pass_on("pk", 2, 0)
    pass_on("mv", 2, 0)
    finish_grad(3)
    pass_on("pv", 2, 0)
    pass_on("mk", 2, 0)
    finish_grad(4)
    send(tail.at[0], tail.at[1], yp, last=True)
    send(tail.at[0], tail.at[3], ym, last=True)
    send(tail.at[0], tail.at[2], y2, last=True)
    got["q1a"]()
    send(q4.at[1, up], q4.at[2, up], yp, last=True)
    got["q3b"]()
    send(q4.at[3, down], q4.at[2, down], ym, last=True)
    for buf in (kk, vt):
        for slot in (1, 7):
            send(buf.at[slot, 0], buf.at[slot, 1], xo, last=True)
    got["g1", 0]()
    forward_grad(0, every, True)
    for name in ("pk", "mv", "pv", "mk"):
        pass_on(name, 2, 1)
    got["g1", 1]()
    forward_grad(1, every, True)
    pass_on("pk", 3, 0)
    pass_on("mv", 3, 0)
    got["g3", 2]()
    forward_grad(2, every, False)
    got["g3", 3]()
    forward_grad(3, every, False)
    pass_on("pk", 3, 1)
    pass_on("mv", 3, 1)
    got["g1", 4]()
    forward_grad(4, up, True)
    got["g3", 4]()
    forward_grad(4, down, False)
    for _ in list_pairs(me, par_buf[...], node_buf[...], plan):
        pass
    for buf in (kk, kt, vt):
        buf[NZ, 0] = jnp.zeros((HD, BLK), BF16)
    wires.finish(zp, sends=False)
    for d in range(NZ):
        for e in range(NX):
            kt[d, e] = kk[d, e].T
    wires.finish(zp)


def gather(q, k, v, o, lse, g, w, par, node):
    blocks = (NZ + 1, NX, HD, BLK)
    return pl.pallas_call(
        gather_kernel,
        out_shape=(
            pltpu.VMEM((NY, HD, ROWS), BF16),
            pltpu.VMEM((NY, HD, ROWS), BF16),
            pltpu.VMEM((NY, 16, BLK), F32),
            pltpu.VMEM(blocks, BF16),
            pltpu.VMEM(blocks, BF16),
            pltpu.VMEM(blocks, BF16),
            pltpu.VMEM((8, 128), jnp.int32),
        ),
        in_specs=[HBM] * 9,
        out_specs=(VMEM,) * 7,
        scratch_shapes=[
            pltpu.VMEM(g.shape, BF16),
            pltpu.VMEM((4, w.shape[0], ROWS), BF16),
            pltpu.VMEM((ROWS, BLK), BF16),
            pltpu.VMEM((GRP, BLK), BF16),
            pltpu.VMEM((ROWS, BLK), BF16),
            pltpu.VMEM((HD, BLK), BF16),
            pltpu.VMEM((1, NODES), jnp.int32),
            pltpu.VMEM((1, NODES), jnp.int32),
            pltpu.VMEM((BLK, ROWS), F32),
        ]
        + [pltpu.VMEM((BLK, ROWS), BF16)] * 6
        + [
            pltpu.VMEM((640, 16, 128), BF16),
            pltpu.SemaphoreType.DMA((12,)),
            pltpu.SemaphoreType.DMA(()),
            pltpu.SemaphoreType.DMA((33,)),
            pltpu.SemaphoreType.DMA(()),
        ],
        compiler_params=pltpu.CompilerParams(
            collective_id=0, has_side_effects=True, vmem_limit_bytes=32 << 20
        ),
        name="gather_and_head_grads",
    )(*place(pltpu.HBM, q, k, v, o, lse, g, w, par, node))


def attend_kernel(plan, q4, g4, tail, kk, kt, vt, dq, dkv):
    ahead = lax.broadcasted_iota(jnp.int32, (BLK, BLK), 0) - lax.broadcasted_iota(
        jnp.int32, (BLK, BLK), 1
    )

    def some(qi, first, count):
        at = [plan[0, qi * KEYS + first + u] for u in range(count)]
        at = [(i // NX, i % NX) for i in at]
        reach = jnp.where((qi == 0) & (first == 0), 0, BLK)
        join = lambda parts, dim: parts[0] if len(parts) == 1 else jnp.concatenate(parts, axis=dim)
        q_c, g_c = q4[qi], g4[qi]
        s_all = jnp.dot(join([kt[i] for i in at], 0), q_c, preferred_element_type=F32)
        dp_all = jnp.dot(join([vt[i] for i in at], 0), g_c, preferred_element_type=F32)
        w_parts, ds_parts = [], []
        for h in range(GRP):
            cols = slice(h * BLK, (h + 1) * BLK)
            p = jnp.exp2(s_all[:, cols] * (SCALE * LOG2E) - tail[qi, h : h + 1, :])
            head = jnp.where(ahead <= reach, p[:BLK], 0.0)
            p = head if count == 1 else jnp.concatenate([head, p[BLK:]], axis=0)
            w_parts.append(p.astype(BF16))
            ds_parts.append((p * (dp_all[:, cols] - tail[qi, 8 + h : 9 + h, :])).astype(BF16))
        w_all, ds_all = join(w_parts, 1), join(ds_parts, 1)
        dq[qi] += jnp.dot(join([kk[i] for i in at], 1), ds_all, preferred_element_type=F32)
        dk_t = lax.dot_general(q_c, ds_all, NT, preferred_element_type=F32)
        dv_t = lax.dot_general(g_c, w_all, NT, preferred_element_type=F32)
        for u, (zi, xi) in enumerate(at):
            dkv[zi, xi, 0] += dk_t[:, u * BLK : (u + 1) * BLK]
            dkv[zi, xi, 1] += dv_t[:, u * BLK : (u + 1) * BLK]

    dq[...] = jnp.zeros_like(dq)
    dkv[...] = jnp.zeros_like(dkv)

    def query_block(qi, carry):
        count = plan[1, qi]
        fours = (count + 1) // 4
        left = count - 4 * fours

        def four(t, carry):
            some(qi, 4 * t, 4)
            return carry

        lax.fori_loop(0, fours, four, 0)

        @pl.when(left == 2)
        def _():
            some(qi, 4 * fours, 2)

        @pl.when(left == 1)
        def _():
            some(qi, 4 * fours, 1)

        return carry

    lax.fori_loop(0, NY, query_block, 0)


def attend(plan, q4, g4, tail, kk, kt, vt):
    return pl.pallas_call(
        attend_kernel,
        out_shape=(
            pltpu.VMEM((NY, HD, ROWS), F32),
            pltpu.VMEM((NZ + 1, NX, 2, HD, BLK), F32),
        ),
        in_specs=[SMEM] + [VMEM] * 6,
        out_specs=(VMEM,) * 2,
        compiler_params=pltpu.CompilerParams(vmem_limit_bytes=32 << 20),
        name="attend_visible_pairs",
    )(plan, *place(pltpu.VMEM, q4, g4, tail, kk, kt, vt))


def scatter_kernel(
    dq, dkv, qp_in, qm_in, own,
    p_out, m_out, p_in, m_in, qp_out, qm_out, q2p_out, q2m_out, qp_half, qm_half, x_out, x_in,
    unit, send_sem, recv_sems, last_sem, vouched,
):
    me = where_am_i()
    yp, ym, zp, zm, xo, xp, xm = (me[n] for n in ("yp", "ym", "zp", "zm", "xo", "xp", "xm"))
    met = hail([yp, ym, zp, zm, xo])
    wires = Wires(send_sem, recv_sems, last_sem, unit)
    send = wires.send
    got = {}
    up, down = pl.ds(0, HALF), pl.ds(HALF, HALF)
    chunks = ((1, 0, True), (1, 1, False), (1, 1, True), (1, 0, False))
    chunks += tuple((0, kv, plus) for _, kv, plus in chunks)

    def stage(left, e, kv, plus):
        slot = NZ - left if plus else left
        out, land = (p_out, p_in) if plus else (m_out, m_in)
        long = plus == (kv == 0)
        value = dkv[slot, e, kv]
        if left < (4 if long else 3):
            got[e, kv, plus]()
            value = value + land[left, e, kv].astype(F32)
        if left == 1:
            if ("x", slot) in got:
                got.pop(("x", slot))()
            got[1, kv, plus]()
            value = value + x_in[1 - plus, kv].astype(F32) + land[1, 1, kv].astype(F32)
        out[left - 1, e, kv] = value.astype(BF16)
        to = (xp if plus else xm) if (left, e) == (2, 1) else (zp if plus else zm)
        got[e, kv, plus] = send(
            out.at[left - 1, e, kv], land.at[left - 1, e, kv], to, left == 1
        )

    q2p_out[...] = dq[2, up].astype(BF16)
    q2m_out[...] = dq[2, down].astype(BF16)
    qp_out[down, :] = dq[3, down].astype(BF16)
    qm_out[up, :] = dq[1, up].astype(BF16)
    met()
    vouch(xo, vouched)
    for e, kv, plus in chunks:
        if plus == (kv == 0):
            stage(4, e, kv, plus)
    got["q2p"] = send(q2p_out, qp_half, yp)
    got["q2m"] = send(q2m_out, qm_half, ym)
    for e, kv, plus in chunks:
        if plus != (kv == 0):
            stage(3, e, kv, plus)
    send(qp_out.at[down], qp_in.at[down], yp, last=True)
    send(qm_out.at[up], qm_in.at[up], ym, last=True)
    for place, slot in enumerate((7, 1, 0)):
        x_out[place] = dkv[slot, 1].astype(BF16)
        got["x", slot] = send(x_out.at[place], x_in.at[place], xo, slot == 0)

    def turn(left):
        for e in (1, 0):
            for e2, kv, plus in chunks:
                step = left if plus == (kv == 0) else left - 1
                if e2 == e and step > e:
                    stage(step, e, kv, plus)

    pl.semaphore_wait(vouched, 1)
    turn(3)
    got["q2p"]()
    qp_out[up, :] = (dq[3, up] + qp_half[...].astype(F32)).astype(BF16)
    send(qp_out.at[up], qp_in.at[up], yp, last=True)
    got["q2m"]()
    qm_out[down, :] = (dq[1, down] + qm_half[...].astype(F32)).astype(BF16)
    send(qm_out.at[down], qm_in.at[down], ym, last=True)
    turn(2)
    turn(1)

    wires.finish(zp, sends=False)
    for kv in (0, 1):
        total = dkv[0, 0, kv] + x_in[2, kv].astype(F32)
        own[kv] = total + p_in[0, 0, kv].astype(F32) + m_in[0, 0, kv].astype(F32)
    wires.finish(zp)


def scatter(dq, dkv):
    ring = (4, NX, 2, HD, BLK)
    wide, half, pair = (HD, ROWS), (HALF, ROWS), (2, HD, BLK)
    return pl.pallas_call(
        scatter_kernel,
        out_shape=(
            pltpu.VMEM(wide, BF16),
            pltpu.VMEM(wide, BF16),
            pltpu.VMEM(pair, F32),
        ),
        in_specs=[VMEM] * 2,
        out_specs=(VMEM,) * 3,
        scratch_shapes=[pltpu.VMEM(ring, BF16)] * 4
        + [pltpu.VMEM(wide, BF16)] * 2
        + [pltpu.VMEM(half, BF16)] * 4
        + [
            pltpu.VMEM((3, *pair), BF16),
            pltpu.VMEM((3, *pair), BF16),
            pltpu.VMEM((400, 16, 128), BF16),
            pltpu.SemaphoreType.DMA(()),
            pltpu.SemaphoreType.DMA((24,)),
            pltpu.SemaphoreType.DMA(()),
            pltpu.SemaphoreType.REGULAR,
        ],
        compiler_params=pltpu.CompilerParams(
            collective_id=1, has_side_effects=True, vmem_limit_bytes=32 << 20
        ),
        name="scatter_sums",
    )(*place(pltpu.VMEM, dq, dkv))


def write_kernel(dq, qp_in, qm_in, own, q_out, k_out, v_out, q_buf, kv_buf, sems):
    copies = []
    for kv, (out, scale) in enumerate(((k_out, SCALE), (v_out, 1.0))):
        kv_buf[kv] = own[kv] * scale
        copies.append(pltpu.make_async_copy(kv_buf.at[kv], out, sems.at[kv]))
        copies[-1].start()
    for h in range(GRP):
        cols = pl.ds(h * BLK, BLK)
        total = dq[0, :, cols] + qp_in[:, cols].astype(F32) + qm_in[:, cols].astype(F32)
        q_buf[pl.ds(h * HD, HD), :] = total * SCALE
    copies.append(pltpu.make_async_copy(q_buf, q_out, sems.at[2]))
    copies[-1].start()
    for copy in copies:
        copy.wait()


def write(dq, qp_in, qm_in, own):
    return pl.pallas_call(
        write_kernel,
        out_shape=(
            jax.ShapeDtypeStruct((ROWS, BLK), F32),
            jax.ShapeDtypeStruct((HD, BLK), F32),
            jax.ShapeDtypeStruct((HD, BLK), F32),
        ),
        in_specs=[VMEM] * 4,
        out_specs=(HBM,) * 3,
        scratch_shapes=[
            pltpu.VMEM((ROWS, BLK), F32),
            pltpu.VMEM((2, HD, BLK), F32),
            pltpu.SemaphoreType.DMA((3,)),
        ],
        name="write_gradients",
    )(*place(pltpu.VMEM, dq, qp_in, qm_in, own))


def body(q, k, v, o, lse, g, w, parents, node_of):
    *rest, plan = gather(q, k, v, o, lse, g, w, parents[None, :], node_of[None, :])
    dq, dkv = attend(plan, *rest)
    return write(dq, *scatter(dq, dkv))


def solution(mesh):
    both, one = P("fsdp", "seq"), P()
    return jax.shard_map(
        body,
        mesh=mesh,
        in_specs=(both,) * 6 + (P("fsdp", None), one, one),
        out_specs=(both,) * 3,
        check_vma=False,
    )
```

```python
import math

import jax
import jax.numpy as jnp
from jax import lax
from jax.experimental import pallas as pl
from jax.experimental.pallas import tpu as pltpu
from jax.sharding import PartitionSpec as P

MESH = pl.DeviceIdType.MESH
HD = 128
BLK = 128
GRP = 5
ROWS = GRP * HD
NX, NZ, NY = 2, 8, 4
NODES = NX * NZ * NY
KEYS = NX * NZ
HALF = HD // 2
SCALE = HD**-0.5
LOG2E = math.log2(math.e)
UNIT = 4096
F32, BF16 = jnp.float32, jnp.bfloat16
HBM = pl.BlockSpec(memory_space=pltpu.HBM)
VMEM = pl.BlockSpec(memory_space=pltpu.VMEM)
SMEM = pl.BlockSpec(memory_space=pltpu.SMEM)
NT = (((1,), (1,)), ((), ()))


def place(space, *arrays):
    return [pltpu.with_memory_space_constraint(array, space) for array in arrays]


def where_am_i():
    s, f = lax.axis_index("seq"), lax.axis_index("fsdp")
    xh, z, y = s // (NZ * NY), (s // NY) % NZ, s % NY
    at = lambda xh, z, y: (xh * NZ + z) * NY + y
    return dict(
        s=s,
        f=f,
        xl=f // 2,
        core=f % 2,
        xh=xh,
        z=z,
        y=y,
        yp=(at(xh, z, (y + 1) % NY), f),
        ym=(at(xh, z, (y + NY - 1) % NY), f),
        y2=(at(xh, z, (y + 2) % NY), f),
        zp=(at(xh, (z + 1) % NZ, y), f),
        zm=(at(xh, (z + NZ - 1) % NZ, y), f),
        zp2=(at(xh, (z + 2) % NZ, y), f),
        zm2=(at(xh, (z + NZ - 2) % NZ, y), f),
        xo=(at(1 - xh, z, y), f),
        xp=(at(1 - xh, (z + 1) % NZ, y), f),
        xm=(at(1 - xh, (z + NZ - 1) % NZ, y), f),
    )


def hail(partners):
    barrier = pltpu.get_barrier_semaphore()
    for partner in partners:
        pl.semaphore_signal(barrier, inc=1, device_id=partner, device_id_type=MESH)
    return lambda: pl.semaphore_wait(barrier, len(partners))


class Wires:
    def __init__(self, send_sem, recv_sems, last_sem, unit):
        self.send_sem, self.recv_sems, self.last_sem, self.unit = send_sem, recv_sems, last_sem, unit
        self.count, self.sent, self.last = 0, 0, 0

    def send(self, src, dst, to, last=False):
        size = math.prod(src.shape) * src.dtype.itemsize // UNIT
        self.sent += size
        if last:
            self.last += size
            recv_sem = self.last_sem
        else:
            recv_sem = self.recv_sems.at[self.count]
            self.count += 1
        copy = pltpu.make_async_remote_copy(
            src_ref=src,
            dst_ref=dst,
            send_sem=self.send_sem,
            recv_sem=recv_sem,
            device_id=to,
            device_id_type=MESH,
        )
        copy.start()
        return None if last else copy.wait_recv

    def finish(self, to, sends=True):
        many = self.unit.at[pl.ds(0, self.sent if sends else self.last)]
        copy = pltpu.make_async_remote_copy(
            src_ref=many,
            dst_ref=many,
            send_sem=self.send_sem,
            recv_sem=self.last_sem,
            device_id=to,
            device_id_type=MESH,
        )
        if sends:
            copy.wait_send()
        else:
            copy.wait_recv()


def vouch(other, sem):
    pl.semaphore_signal(sem, inc=1, device_id=other, device_id_type=MESH)


def list_pairs(me, parents, node_of, plan):
    iota = lambda dim: lax.broadcasted_iota(jnp.int32, (NODES, NODES), dim)
    hot = lambda mask: jnp.where(mask, 1.0, 0.0).astype(BF16)
    dot = lambda a, b: jnp.dot(a, b, preferred_element_type=F32)
    rows, cols = iota(0), iota(1)
    reach = hot((rows == parents) | (rows == cols))
    for _ in range(NODES.bit_length()):
        reach = hot(dot(reach, reach) > 0.5)
        yield
    placed = hot(rows == node_of)
    k, q = cols % KEYS, cols // KEYS
    k_xh = jnp.where(k % NX > 0, 1 - me["xh"], me["xh"])
    k_z = (me["z"] + NZ - k // NX) % NZ
    q_y = (me["y"] + NY - q) % NY
    node_k = dot(placed, hot(rows == (k_xh * NZ + k_z) * NY + me["y"]))
    node_q = dot(placed, hot(rows == (me["xh"] * NZ + me["z"]) * NY + q_y))
    yield
    above = dot(reach, node_q.astype(BF16))
    seen = hot(jnp.sum(node_k * above, axis=0, keepdims=True) > 0.5)
    yield
    before = dot(seen, hot((rows < cols) & (rows // KEYS == q)))
    pair = lax.broadcasted_iota(jnp.int32, (1, NODES), 1)
    place = (pair // KEYS * KEYS).astype(F32) + before
    spot = hot((rows.astype(F32) == place) & (seen.astype(F32) > 0.5))
    from_end = (pair % KEYS - KEYS).astype(F32)
    order = lax.dot_general(from_end.astype(BF16), spot, NT, preferred_element_type=F32) + KEYS
    counts = dot(seen, hot(rows // KEYS == cols))
    plan[0:1, 0:NODES] = order.astype(jnp.int32)
    plan[1:2, 0:NODES] = counts.astype(jnp.int32)


def gather_kernel(
    q_ref, k_ref, v_ref, o_ref, lse_ref, g_ref, w_ref, par_ref, node_ref,
    q4, g4, tail, kk, kt, vt, plan,
    g_buf, w_buf, o_buf, lse_buf, q_buf, v_buf, par_buf, node_buf,
    part, out_a, in_a, sum_b, in_b, out_c, in_c,
    unit, local_sems, send_sem, recv_sems, last_sem,
):
    me = where_am_i()
    xl, core = me["xl"], me["core"]
    sib = (me["s"], 2 * xl + 1 - core)
    xlo = (me["s"], 2 * (1 - xl) + core)
    near = [me[n] for n in ("yp", "ym", "y2", "zp", "zm", "zp2", "zm2", "xo")]
    yp, ym, y2, zp, zm, zp2, zm2, xo = near
    met = hail(near + [sib, xlo])

    def fetch(src, dst, index):
        copy = pltpu.make_async_copy(src, dst, local_sems.at[index])
        copy.start()
        return copy.wait

    get_k = fetch(k_ref, kk.at[0, 0], 0)
    get_v = fetch(v_ref, v_buf, 1)
    get_g = fetch(g_ref, g_buf, 2)
    get_w = []
    for i, (a, b) in enumerate(((1 - xl, 1 - core), (1 - xl, core), (xl, 1 - core), (xl, core))):
        first = pl.multiple_of((2 * a + b) * ROWS, ROWS)
        get_w.append(fetch(w_ref.at[:, pl.ds(first, ROWS)], w_buf.at[i], 3 + i))
        if i == 0:
            get_q = fetch(q_ref, q_buf, 7)
    get_lse = fetch(lse_ref, lse_buf, 8)
    get_par = fetch(par_ref, par_buf, 9)
    get_node = fetch(node_ref, node_buf, 10)
    get_o = fetch(o_ref, o_buf, 11)

    got = {}
    up, down = pl.ds(0, HALF), pl.ds(HALF, HALF)
    wires = Wires(send_sem, recv_sems, last_sem, unit)
    send = wires.send

    get_v()
    vt[0, 0] = v_buf[...].T
    get_k()
    get_q()
    for h in range(GRP):
        q4[0, :, pl.ds(h * BLK, BLK)] = q_buf[pl.ds(h * HD, HD), :]
    get_g()
    gt = g_buf[...].T

    def partial_sum(i):
        get_w[i]()
        return jnp.dot(gt, w_buf[i], preferred_element_type=F32)

    out_a[...] = partial_sum(0).astype(BF16)
    met()
    got["a"] = send(out_a, in_a, sib)
    got["xk"] = send(kk.at[0, 0], kk.at[0, 1], xo)
    got["xv"] = send(vt.at[0, 0], vt.at[0, 1], xo)
    got["pk", 0] = send(kk.at[0, 0], kk.at[1, 0], zp)
    got["mv", 0] = send(vt.at[0, 0], vt.at[7, 0], zm)
    got["pv", 0] = send(vt.at[0, 0], vt.at[1, 0], zp)
    got["mk", 0] = send(kk.at[0, 0], kk.at[7, 0], zm)
    got["q1a"] = send(q4.at[0, up], q4.at[1, up], yp)
    got["q3b"] = send(q4.at[0, down], q4.at[3, down], ym)
    send(q4.at[0, down], q4.at[1, down], yp, last=True)
    send(q4.at[0, up], q4.at[3, up], ym, last=True)
    part[...] = partial_sum(1)
    got["a"]()
    for h in range(GRP):
        cols = pl.ds(h * BLK, BLK)
        sum_b[:, cols] = (part[:, cols] + in_a[:, cols].astype(F32)).astype(BF16)
        got["b", h] = send(sum_b.at[:, cols], in_b.at[:, cols], xlo)
    out_c[...] = partial_sum(2).astype(BF16)
    got["c"] = send(out_c, in_c, sib)
    part[...] = partial_sum(3)

    def pass_on(name, d, e):
        buf = kk if name[1] == "k" else vt
        last = d == 3 or d == 2 and name in ("pv", "mk")
        got[name, e]()
        here, there, to = (d, d + 1, zp) if name[0] == "p" else (NZ - d, NZ - d - 1, zm)
        if (d, e) == (2, 1):
            last = True
            if name in ("pk", "mv"):
                send(buf.at[here, 1], buf.at[4, 1], zp2 if name == "pk" else zm2, last=True)
        got[name, e] = send(buf.at[here, e], buf.at[there, e], to, last)

    def finish_grad(h):
        cols = pl.ds(h * BLK, BLK)
        got["b", h]()
        grad = part[:, cols] + in_c[:, cols].astype(F32) + in_b[:, cols].astype(F32)
        grad = grad.T.astype(BF16)
        g4[0, :, cols] = grad
        got["g1", h] = send(g4.at[0, :, cols], g4.at[1, :, cols], yp, h in (2, 3))
        got["g3", h] = send(g4.at[0, :, cols], g4.at[3, :, cols], ym, h in (0, 1))
        product = grad.astype(F32) * o_buf[pl.ds(h * HD, HD), :].astype(F32)
        tail[0, 8 + h : 9 + h, :] = jnp.sum(product, axis=0, keepdims=True)

    def forward_grad(h, rows, plus):
        cols = pl.ds(h * BLK, BLK)
        slot, to = (1, yp) if plus else (3, ym)
        send(g4.at[slot, rows, cols], g4.at[2, rows, cols], to, last=True)

    every = pl.ds(0, HD)
    get_par()
    get_node()
    get_lse()
    get_o()
    tail[0, 0:GRP, :] = lse_buf[...].astype(F32) * LOG2E
    got["c"]()
    for name in ("pk", "mv", "pv", "mk"):
        pass_on(name, 1, 0)
    got["xk"]()
    got["pk", 1] = send(kk.at[0, 1], kk.at[2, 1], zp2)
    got["mk", 1] = send(kk.at[0, 1], kk.at[6, 1], zm2)
    got["xv"]()
    got["mv", 1] = send(vt.at[0, 1], vt.at[6, 1], zm2)
    got["pv", 1] = send(vt.at[0, 1], vt.at[2, 1], zp2)
    finish_grad(0)
    finish_grad(1)
    finish_grad(2)
    pass_on("pk", 2, 0)
    pass_on("mv", 2, 0)
    finish_grad(3)
    pass_on("pv", 2, 0)
    pass_on("mk", 2, 0)
    finish_grad(4)
    send(tail.at[0], tail.at[1], yp, last=True)
    send(tail.at[0], tail.at[3], ym, last=True)
    send(tail.at[0], tail.at[2], y2, last=True)
    got["q1a"]()
    send(q4.at[1, up], q4.at[2, up], yp, last=True)
    got["q3b"]()
    send(q4.at[3, down], q4.at[2, down], ym, last=True)
    for buf in (kk, vt):
        for slot in (1, 7):
            send(buf.at[slot, 0], buf.at[slot, 1], xo, last=True)
    got["g1", 0]()
    forward_grad(0, every, True)
    for name in ("pk", "mv", "pv", "mk"):
        pass_on(name, 2, 1)
    got["g1", 1]()
    forward_grad(1, every, True)
    pass_on("pk", 3, 0)
    pass_on("mv", 3, 0)
    got["g3", 2]()
    forward_grad(2, every, False)
    got["g3", 3]()
    forward_grad(3, every, False)
    got["g1", 4]()
    forward_grad(4, up, True)
    got["g3", 4]()
    forward_grad(4, down, False)
    for _ in list_pairs(me, par_buf[...], node_buf[...], plan):
        pass
    for buf in (kk, kt, vt):
        buf[NZ, 0] = jnp.zeros((HD, BLK), BF16)
    wires.finish(zp, sends=False)
    for d in range(NZ):
        for e in range(NX):
            kt[d, e] = kk[d, e].T
    wires.finish(zp)


def gather(q, k, v, o, lse, g, w, par, node):
    blocks = (NZ + 1, NX, HD, BLK)
    return pl.pallas_call(
        gather_kernel,
        out_shape=(
            pltpu.VMEM((NY, HD, ROWS), BF16),
            pltpu.VMEM((NY, HD, ROWS), BF16),
            pltpu.VMEM((NY, 16, BLK), F32),
            pltpu.VMEM(blocks, BF16),
            pltpu.VMEM(blocks, BF16),
            pltpu.VMEM(blocks, BF16),
            pltpu.VMEM((8, 128), jnp.int32),
        ),
        in_specs=[HBM] * 9,
        out_specs=(VMEM,) * 7,
        scratch_shapes=[
            pltpu.VMEM(g.shape, BF16),
            pltpu.VMEM((4, w.shape[0], ROWS), BF16),
            pltpu.VMEM((ROWS, BLK), BF16),
            pltpu.VMEM((GRP, BLK), BF16),
            pltpu.VMEM((ROWS, BLK), BF16),
            pltpu.VMEM((HD, BLK), BF16),
            pltpu.VMEM((1, NODES), jnp.int32),
            pltpu.VMEM((1, NODES), jnp.int32),
            pltpu.VMEM((BLK, ROWS), F32),
        ]
        + [pltpu.VMEM((BLK, ROWS), BF16)] * 6
        + [
            pltpu.VMEM((640, 16, 128), BF16),
            pltpu.SemaphoreType.DMA((12,)),
            pltpu.SemaphoreType.DMA(()),
            pltpu.SemaphoreType.DMA((31,)),
            pltpu.SemaphoreType.DMA(()),
        ],
        compiler_params=pltpu.CompilerParams(
            collective_id=0, has_side_effects=True, vmem_limit_bytes=32 << 20
        ),
        name="gather_and_head_grads",
    )(*place(pltpu.HBM, q, k, v, o, lse, g, w, par, node))


def attend_kernel(plan, q4, g4, tail, kk, kt, vt, dq, dkv):
    ahead = lax.broadcasted_iota(jnp.int32, (BLK, BLK), 0) - lax.broadcasted_iota(
        jnp.int32, (BLK, BLK), 1
    )

    def some(qi, first, count):
        at = [plan[0, qi * KEYS + first + u] for u in range(count)]
        at = [(i // NX, i % NX) for i in at]
        reach = jnp.where((qi == 0) & (first == 0), 0, BLK)
        join = lambda parts, dim: parts[0] if len(parts) == 1 else jnp.concatenate(parts, axis=dim)
        q_c, g_c = q4[qi], g4[qi]
        s_all = jnp.dot(join([kt[i] for i in at], 0), q_c, preferred_element_type=F32)
        dp_all = jnp.dot(join([vt[i] for i in at], 0), g_c, preferred_element_type=F32)
        w_parts, ds_parts = [], []
        for h in range(GRP):
            cols = slice(h * BLK, (h + 1) * BLK)
            p = jnp.exp2(s_all[:, cols] * (SCALE * LOG2E) - tail[qi, h : h + 1, :])
            head = jnp.where(ahead <= reach, p[:BLK], 0.0)
            p = head if count == 1 else jnp.concatenate([head, p[BLK:]], axis=0)
            w_parts.append(p.astype(BF16))
            ds_parts.append((p * (dp_all[:, cols] - tail[qi, 8 + h : 9 + h, :])).astype(BF16))
        w_all, ds_all = join(w_parts, 1), join(ds_parts, 1)
        dq[qi] += jnp.dot(join([kk[i] for i in at], 1), ds_all, preferred_element_type=F32)
        dk_t = lax.dot_general(q_c, ds_all, NT, preferred_element_type=F32)
        dv_t = lax.dot_general(g_c, w_all, NT, preferred_element_type=F32)
        for u, (zi, xi) in enumerate(at):
            dkv[zi, xi, 0] += dk_t[:, u * BLK : (u + 1) * BLK]
            dkv[zi, xi, 1] += dv_t[:, u * BLK : (u + 1) * BLK]

    dq[...] = jnp.zeros_like(dq)
    dkv[...] = jnp.zeros_like(dkv)

    def query_block(qi, carry):
        count = plan[1, qi]
        fours = (count + 1) // 4
        left = count - 4 * fours

        def four(t, carry):
            some(qi, 4 * t, 4)
            return carry

        lax.fori_loop(0, fours, four, 0)

        @pl.when(left == 2)
        def _():
            some(qi, 4 * fours, 2)

        @pl.when(left == 1)
        def _():
            some(qi, 4 * fours, 1)

        return carry

    lax.fori_loop(0, NY, query_block, 0)


def attend(plan, q4, g4, tail, kk, kt, vt):
    return pl.pallas_call(
        attend_kernel,
        out_shape=(
            pltpu.VMEM((NY, HD, ROWS), F32),
            pltpu.VMEM((NZ + 1, NX, 2, HD, BLK), F32),
        ),
        in_specs=[SMEM] + [VMEM] * 6,
        out_specs=(VMEM,) * 2,
        compiler_params=pltpu.CompilerParams(vmem_limit_bytes=32 << 20),
        name="attend_visible_pairs",
    )(plan, *place(pltpu.VMEM, q4, g4, tail, kk, kt, vt))


def scatter_kernel(
    dq, dkv, qp_in, qm_in, own,
    p_out, m_out, p_in, m_in, qp_out, qm_out, q2p_out, q2m_out, qp_half, qm_half, x_out, x_in,
    unit, send_sem, recv_sems, last_sem, vouched,
):
    me = where_am_i()
    yp, ym, zp, zm, xo, xp, xm = (me[n] for n in ("yp", "ym", "zp", "zm", "xo", "xp", "xm"))
    met = hail([yp, ym, zp, zm, xo])
    wires = Wires(send_sem, recv_sems, last_sem, unit)
    send = wires.send
    got = {}
    up, down = pl.ds(0, HALF), pl.ds(HALF, HALF)
    chunks = ((1, 0, True), (1, 1, False), (1, 1, True), (1, 0, False))
    chunks += tuple((0, kv, plus) for _, kv, plus in chunks)

    def stage(left, e, kv, plus):
        slot = NZ - left if plus else left
        out, land = (p_out, p_in) if plus else (m_out, m_in)
        long = plus == (kv == 0)
        value = dkv[slot, e, kv]
        if left < (4 if long else 3):
            got[e, kv, plus]()
            value = value + land[left, e, kv].astype(F32)
        if left == 1:
            if ("x", slot) in got:
                got.pop(("x", slot))()
            got[1, kv, plus]()
            value = value + x_in[1 - plus, kv].astype(F32) + land[1, 1, kv].astype(F32)
        out[left - 1, e, kv] = value.astype(BF16)
        to = (xp if plus else xm) if (left, e) == (2, 1) else (zp if plus else zm)
        got[e, kv, plus] = send(
            out.at[left - 1, e, kv], land.at[left - 1, e, kv], to, left == 1
        )

    q2p_out[...] = dq[2, up].astype(BF16)
    q2m_out[...] = dq[2, down].astype(BF16)
    qp_out[down, :] = dq[3, down].astype(BF16)
    qm_out[up, :] = dq[1, up].astype(BF16)
    met()
    vouch(xo, vouched)
    for e, kv, plus in chunks:
        if plus == (kv == 0):
            stage(4, e, kv, plus)
    got["q2p"] = send(q2p_out, qp_half, yp)
    got["q2m"] = send(q2m_out, qm_half, ym)
    for e, kv, plus in chunks:
        if plus != (kv == 0):
            stage(3, e, kv, plus)
    send(qp_out.at[down], qp_in.at[down], yp, last=True)
    send(qm_out.at[up], qm_in.at[up], ym, last=True)
    for place, slot in enumerate((7, 1, 0)):
        x_out[place] = dkv[slot, 1].astype(BF16)
        got["x", slot] = send(x_out.at[place], x_in.at[place], xo, slot == 0)

    def turn(left):
        for e in (1, 0):
            for e2, kv, plus in chunks:
                step = left if plus == (kv == 0) else left - 1
                if e2 == e and step > e:
                    stage(step, e, kv, plus)

    pl.semaphore_wait(vouched, 1)
    turn(3)
    got["q2p"]()
    qp_out[up, :] = (dq[3, up] + qp_half[...].astype(F32)).astype(BF16)
    send(qp_out.at[up], qp_in.at[up], yp, last=True)
    got["q2m"]()
    qm_out[down, :] = (dq[1, down] + qm_half[...].astype(F32)).astype(BF16)
    send(qm_out.at[down], qm_in.at[down], ym, last=True)
    turn(2)
    turn(1)

    wires.finish(zp, sends=False)
    for kv in (0, 1):
        total = dkv[0, 0, kv] + x_in[2, kv].astype(F32)
        own[kv] = total + p_in[0, 0, kv].astype(F32) + m_in[0, 0, kv].astype(F32)
    wires.finish(zp)


def scatter(dq, dkv):
    ring = (4, NX, 2, HD, BLK)
    wide, half, pair = (HD, ROWS), (HALF, ROWS), (2, HD, BLK)
    return pl.pallas_call(
        scatter_kernel,
        out_shape=(
            pltpu.VMEM(wide, BF16),
            pltpu.VMEM(wide, BF16),
            pltpu.VMEM(pair, F32),
        ),
        in_specs=[VMEM] * 2,
        out_specs=(VMEM,) * 3,
        scratch_shapes=[pltpu.VMEM(ring, BF16)] * 4
        + [pltpu.VMEM(wide, BF16)] * 2
        + [pltpu.VMEM(half, BF16)] * 4
        + [
            pltpu.VMEM((3, *pair), BF16),
            pltpu.VMEM((3, *pair), BF16),
            pltpu.VMEM((400, 16, 128), BF16),
            pltpu.SemaphoreType.DMA(()),
            pltpu.SemaphoreType.DMA((24,)),
            pltpu.SemaphoreType.DMA(()),
            pltpu.SemaphoreType.REGULAR,
        ],
        compiler_params=pltpu.CompilerParams(
            collective_id=1, has_side_effects=True, vmem_limit_bytes=32 << 20
        ),
        name="scatter_sums",
    )(*place(pltpu.VMEM, dq, dkv))


def write_kernel(dq, qp_in, qm_in, own, q_out, k_out, v_out, q_buf, kv_buf, sems):
    copies = []
    for kv, (out, scale) in enumerate(((k_out, SCALE), (v_out, 1.0))):
        kv_buf[kv] = own[kv] * scale
        copies.append(pltpu.make_async_copy(kv_buf.at[kv], out, sems.at[kv]))
        copies[-1].start()
    for h in range(GRP):
        cols = pl.ds(h * BLK, BLK)
        total = dq[0, :, cols] + qp_in[:, cols].astype(F32) + qm_in[:, cols].astype(F32)
        q_buf[pl.ds(h * HD, HD), :] = total * SCALE
    copies.append(pltpu.make_async_copy(q_buf, q_out, sems.at[2]))
    copies[-1].start()
    for copy in copies:
        copy.wait()


def write(dq, qp_in, qm_in, own):
    return pl.pallas_call(
        write_kernel,
        out_shape=(
            jax.ShapeDtypeStruct((ROWS, BLK), F32),
            jax.ShapeDtypeStruct((HD, BLK), F32),
            jax.ShapeDtypeStruct((HD, BLK), F32),
        ),
        in_specs=[VMEM] * 4,
        out_specs=(HBM,) * 3,
        scratch_shapes=[
            pltpu.VMEM((ROWS, BLK), F32),
            pltpu.VMEM((2, HD, BLK), F32),
            pltpu.SemaphoreType.DMA((3,)),
        ],
        name="write_gradients",
    )(*place(pltpu.VMEM, dq, qp_in, qm_in, own))


def body(q, k, v, o, lse, g, w, parents, node_of):
    *rest, plan = gather(q, k, v, o, lse, g, w, parents[None, :], node_of[None, :])
    dq, dkv = attend(plan, *rest)
    return write(dq, *scatter(dq, dkv))


def solution(mesh):
    both, one = P("fsdp", "seq"), P()
    return jax.shard_map(
        body,
        mesh=mesh,
        in_specs=(both,) * 6 + (P("fsdp", None), one, one),
        out_specs=(both,) * 3,
        check_vma=False,
    )
```

```python
import math

import jax
import jax.numpy as jnp
from jax import lax
from jax.experimental import pallas as pl
from jax.experimental.pallas import tpu as pltpu
from jax.sharding import PartitionSpec as P

MESH = pl.DeviceIdType.MESH
HD = 128
BLK = 128
GRP = 5
ROWS = GRP * HD
NX, NZ, NY = 2, 8, 4
NODES = NX * NZ * NY
KEYS = NX * NZ
HALF = HD // 2
SCALE = HD**-0.5
LOG2E = math.log2(math.e)
UNIT = 4096
F32, BF16 = jnp.float32, jnp.bfloat16
HBM = pl.BlockSpec(memory_space=pltpu.HBM)
VMEM = pl.BlockSpec(memory_space=pltpu.VMEM)
SMEM = pl.BlockSpec(memory_space=pltpu.SMEM)
NT = (((1,), (1,)), ((), ()))


def place(space, *arrays):
    return [pltpu.with_memory_space_constraint(array, space) for array in arrays]


def where_am_i():
    s, f = lax.axis_index("seq"), lax.axis_index("fsdp")
    xh, z, y = s // (NZ * NY), (s // NY) % NZ, s % NY
    at = lambda xh, z, y: (xh * NZ + z) * NY + y
    return dict(
        s=s,
        f=f,
        xl=f // 2,
        core=f % 2,
        xh=xh,
        z=z,
        y=y,
        yp=(at(xh, z, (y + 1) % NY), f),
        ym=(at(xh, z, (y + NY - 1) % NY), f),
        y2=(at(xh, z, (y + 2) % NY), f),
        zp=(at(xh, (z + 1) % NZ, y), f),
        zm=(at(xh, (z + NZ - 1) % NZ, y), f),
        zp2=(at(xh, (z + 2) % NZ, y), f),
        zm2=(at(xh, (z + NZ - 2) % NZ, y), f),
        xo=(at(1 - xh, z, y), f),
        xp=(at(1 - xh, (z + 1) % NZ, y), f),
        xm=(at(1 - xh, (z + NZ - 1) % NZ, y), f),
    )


def hail(partners):
    barrier = pltpu.get_barrier_semaphore()
    for partner in partners:
        pl.semaphore_signal(barrier, inc=1, device_id=partner, device_id_type=MESH)
    return lambda: pl.semaphore_wait(barrier, len(partners))


class Wires:
    def __init__(self, send_sem, recv_sems, last_sem, unit):
        self.send_sem, self.recv_sems, self.last_sem, self.unit = send_sem, recv_sems, last_sem, unit
        self.count, self.sent, self.last = 0, 0, 0

    def send(self, src, dst, to, last=False):
        size = math.prod(src.shape) * src.dtype.itemsize // UNIT
        self.sent += size
        if last:
            self.last += size
            recv_sem = self.last_sem
        else:
            recv_sem = self.recv_sems.at[self.count]
            self.count += 1
        copy = pltpu.make_async_remote_copy(
            src_ref=src,
            dst_ref=dst,
            send_sem=self.send_sem,
            recv_sem=recv_sem,
            device_id=to,
            device_id_type=MESH,
        )
        copy.start()
        return None if last else copy.wait_recv

    def finish(self, to, sends=True):
        many = self.unit.at[pl.ds(0, self.sent if sends else self.last)]
        copy = pltpu.make_async_remote_copy(
            src_ref=many,
            dst_ref=many,
            send_sem=self.send_sem,
            recv_sem=self.last_sem,
            device_id=to,
            device_id_type=MESH,
        )
        if sends:
            copy.wait_send()
        else:
            copy.wait_recv()


def vouch(other, sem):
    pl.semaphore_signal(sem, inc=1, device_id=other, device_id_type=MESH)


def list_pairs(me, parents, node_of, plan):
    iota = lambda dim: lax.broadcasted_iota(jnp.int32, (NODES, NODES), dim)
    hot = lambda mask: jnp.where(mask, 1.0, 0.0).astype(BF16)
    dot = lambda a, b: jnp.dot(a, b, preferred_element_type=F32)
    rows, cols = iota(0), iota(1)
    reach = hot((rows == parents) | (rows == cols))
    for _ in range(NODES.bit_length()):
        reach = hot(dot(reach, reach) > 0.5)
        yield
    placed = hot(rows == node_of)
    k, q = cols % KEYS, cols // KEYS
    k_xh = jnp.where(k % NX > 0, 1 - me["xh"], me["xh"])
    k_z = (me["z"] + NZ - k // NX) % NZ
    q_y = (me["y"] + NY - q) % NY
    node_k = dot(placed, hot(rows == (k_xh * NZ + k_z) * NY + me["y"]))
    node_q = dot(placed, hot(rows == (me["xh"] * NZ + me["z"]) * NY + q_y))
    yield
    above = dot(reach, node_q.astype(BF16))
    seen = hot(jnp.sum(node_k * above, axis=0, keepdims=True) > 0.5)
    yield
    before = dot(seen, hot((rows < cols) & (rows // KEYS == q)))
    pair = lax.broadcasted_iota(jnp.int32, (1, NODES), 1)
    place = (pair // KEYS * KEYS).astype(F32) + before
    spot = hot((rows.astype(F32) == place) & (seen.astype(F32) > 0.5))
    from_end = (pair % KEYS - KEYS).astype(F32)
    order = lax.dot_general(from_end.astype(BF16), spot, NT, preferred_element_type=F32) + KEYS
    counts = dot(seen, hot(rows // KEYS == cols))
    plan[0:1, 0:NODES] = order.astype(jnp.int32)
    plan[1:2, 0:NODES] = counts.astype(jnp.int32)


def gather_kernel(
    q_ref, k_ref, v_ref, o_ref, lse_ref, g_ref, w_ref, par_ref, node_ref,
    q4, g4, tail, kk, kt, vt, dq, dkv, plan,
    g_buf, w_buf, o_buf, lse_buf, q_buf, v_buf, par_buf, node_buf,
    part, out_a, in_a, sum_b, in_b, out_c, in_c,
    unit, local_sems, send_sem, recv_sems, last_sem,
):
    me = where_am_i()
    xl, core = me["xl"], me["core"]
    sib = (me["s"], 2 * xl + 1 - core)
    xlo = (me["s"], 2 * (1 - xl) + core)
    near = [me[n] for n in ("yp", "ym", "y2", "zp", "zm", "zp2", "zm2", "xo")]
    yp, ym, y2, zp, zm, zp2, zm2, xo = near
    met = hail(near + [sib, xlo])

    def fetch(src, dst, index):
        copy = pltpu.make_async_copy(src, dst, local_sems.at[index])
        copy.start()
        return copy.wait

    get_k = fetch(k_ref, kk.at[0, 0], 0)
    get_v = fetch(v_ref, v_buf, 1)
    get_g = fetch(g_ref, g_buf, 2)
    get_w = []
    for i, (a, b) in enumerate(((1 - xl, 1 - core), (1 - xl, core), (xl, 1 - core), (xl, core))):
        first = pl.multiple_of((2 * a + b) * ROWS, ROWS)
        get_w.append(fetch(w_ref.at[:, pl.ds(first, ROWS)], w_buf.at[i], 3 + i))
        if i == 0:
            get_q = fetch(q_ref, q_buf, 7)
    get_lse = fetch(lse_ref, lse_buf, 8)
    get_par = fetch(par_ref, par_buf, 9)
    get_node = fetch(node_ref, node_buf, 10)
    get_o = fetch(o_ref, o_buf, 11)

    got = {}
    up, down = pl.ds(0, HALF), pl.ds(HALF, HALF)
    wires = Wires(send_sem, recv_sems, last_sem, unit)
    send = wires.send

    get_v()
    vt[0, 0] = v_buf[...].T
    get_k()
    get_q()
    for h in range(GRP):
        q4[0, :, pl.ds(h * BLK, BLK)] = q_buf[pl.ds(h * HD, HD), :]
    get_g()
    gt = g_buf[...].T

    def partial_sum(i):
        get_w[i]()
        return jnp.dot(gt, w_buf[i], preferred_element_type=F32)

    out_a[...] = partial_sum(0).astype(BF16)
    met()
    got["a"] = send(out_a, in_a, sib)
    got["xk"] = send(kk.at[0, 0], kk.at[0, 1], xo)
    got["xv"] = send(vt.at[0, 0], vt.at[0, 1], xo)
    got["pk", 0] = send(kk.at[0, 0], kk.at[1, 0], zp)
    got["mv", 0] = send(vt.at[0, 0], vt.at[7, 0], zm)
    got["pv", 0] = send(vt.at[0, 0], vt.at[1, 0], zp)
    got["mk", 0] = send(kk.at[0, 0], kk.at[7, 0], zm)
    got["q1a"] = send(q4.at[0, up], q4.at[1, up], yp)
    got["q3b"] = send(q4.at[0, down], q4.at[3, down], ym)
    send(q4.at[0, down], q4.at[1, down], yp, last=True)
    send(q4.at[0, up], q4.at[3, up], ym, last=True)
    part[...] = partial_sum(1)
    got["a"]()
    for h in range(GRP):
        cols = pl.ds(h * BLK, BLK)
        sum_b[:, cols] = (part[:, cols] + in_a[:, cols].astype(F32)).astype(BF16)
        got["b", h] = send(sum_b.at[:, cols], in_b.at[:, cols], xlo)
    out_c[...] = partial_sum(2).astype(BF16)
    got["c"] = send(out_c, in_c, sib)
    part[...] = partial_sum(3)

    def pass_on(name, d, e):
        buf = kk if name[1] == "k" else vt
        last = d == 3 or d == 2 and name in ("pv", "mk")
        got[name, e]()
        here, there, to = (d, d + 1, zp) if name[0] == "p" else (NZ - d, NZ - d - 1, zm)
        if (d, e) == (2, 1):
            last = True
            if name in ("pk", "mv"):
                send(buf.at[here, 1], buf.at[4, 1], zp2 if name == "pk" else zm2, last=True)
        got[name, e] = send(buf.at[here, e], buf.at[there, e], to, last)

    def finish_grad(h):
        cols = pl.ds(h * BLK, BLK)
        got["b", h]()
        grad = part[:, cols] + in_c[:, cols].astype(F32) + in_b[:, cols].astype(F32)
        grad = grad.T.astype(BF16)
        g4[0, :, cols] = grad
        got["g1", h] = send(g4.at[0, :, cols], g4.at[1, :, cols], yp, h in (2, 3))
        got["g3", h] = send(g4.at[0, :, cols], g4.at[3, :, cols], ym, h in (0, 1))
        product = grad.astype(F32) * o_buf[pl.ds(h * HD, HD), :].astype(F32)
        tail[0, 8 + h : 9 + h, :] = jnp.sum(product, axis=0, keepdims=True)

    def forward_grad(h, rows, plus):
        cols = pl.ds(h * BLK, BLK)
        slot, to = (1, yp) if plus else (3, ym)
        send(g4.at[slot, rows, cols], g4.at[2, rows, cols], to, last=True)

    every = pl.ds(0, HD)
    get_par()
    get_node()
    get_lse()
    get_o()
    tail[0, 0:GRP, :] = lse_buf[...].astype(F32) * LOG2E
    got["c"]()
    for name in ("pk", "mv", "pv", "mk"):
        pass_on(name, 1, 0)
    got["xk"]()
    got["pk", 1] = send(kk.at[0, 1], kk.at[2, 1], zp2)
    got["mk", 1] = send(kk.at[0, 1], kk.at[6, 1], zm2)
    got["xv"]()
    got["mv", 1] = send(vt.at[0, 1], vt.at[6, 1], zm2)
    got["pv", 1] = send(vt.at[0, 1], vt.at[2, 1], zp2)
    finish_grad(0)
    finish_grad(1)
    finish_grad(2)
    pass_on("pk", 2, 0)
    pass_on("mv", 2, 0)
    finish_grad(3)
    for buf in (kk, vt):
        for slot in (1, 7):
            send(buf.at[slot, 0], buf.at[slot, 1], xo, last=True)
    pass_on("pv", 2, 0)
    pass_on("mk", 2, 0)
    finish_grad(4)
    send(tail.at[0], tail.at[1], yp, last=True)
    send(tail.at[0], tail.at[3], ym, last=True)
    send(tail.at[0], tail.at[2], y2, last=True)
    got["q1a"]()
    send(q4.at[1, up], q4.at[2, up], yp, last=True)
    got["q3b"]()
    send(q4.at[3, down], q4.at[2, down], ym, last=True)
    got["g1", 0]()
    forward_grad(0, every, True)
    for name in ("pk", "mv", "pv", "mk"):
        pass_on(name, 2, 1)
    got["g1", 1]()
    forward_grad(1, every, True)
    pass_on("pk", 3, 0)
    pass_on("mv", 3, 0)
    got["g3", 2]()
    forward_grad(2, every, False)
    got["g3", 3]()
    forward_grad(3, every, False)
    got["g1", 4]()
    forward_grad(4, up, True)
    got["g3", 4]()
    forward_grad(4, down, False)
    dq[...] = jnp.zeros_like(dq)
    dkv[...] = jnp.zeros_like(dkv)
    for _ in list_pairs(me, par_buf[...], node_buf[...], plan):
        pass
    for buf in (kk, kt, vt):
        buf[NZ, 0] = jnp.zeros((HD, BLK), BF16)
    wires.finish(zp, sends=False)
    for d in range(NZ):
        for e in range(NX):
            kt[d, e] = kk[d, e].T
    wires.finish(zp)


def gather(q, k, v, o, lse, g, w, par, node):
    blocks = (NZ + 1, NX, HD, BLK)
    return pl.pallas_call(
        gather_kernel,
        out_shape=(
            pltpu.VMEM((NY, HD, ROWS), BF16),
            pltpu.VMEM((NY, HD, ROWS), BF16),
            pltpu.VMEM((NY, 16, BLK), F32),
            pltpu.VMEM(blocks, BF16),
            pltpu.VMEM(blocks, BF16),
            pltpu.VMEM(blocks, BF16),
            pltpu.VMEM((NY, HD, ROWS), F32),
            pltpu.VMEM((NZ + 1, NX, 2, HD, BLK), F32),
            pltpu.VMEM((8, 128), jnp.int32),
        ),
        in_specs=[HBM] * 9,
        out_specs=(VMEM,) * 9,
        scratch_shapes=[
            pltpu.VMEM(g.shape, BF16),
            pltpu.VMEM((4, w.shape[0], ROWS), BF16),
            pltpu.VMEM((ROWS, BLK), BF16),
            pltpu.VMEM((GRP, BLK), BF16),
            pltpu.VMEM((ROWS, BLK), BF16),
            pltpu.VMEM((HD, BLK), BF16),
            pltpu.VMEM((1, NODES), jnp.int32),
            pltpu.VMEM((1, NODES), jnp.int32),
            pltpu.VMEM((BLK, ROWS), F32),
        ]
        + [pltpu.VMEM((BLK, ROWS), BF16)] * 6
        + [
            pltpu.VMEM((640, 16, 128), BF16),
            pltpu.SemaphoreType.DMA((12,)),
            pltpu.SemaphoreType.DMA(()),
            pltpu.SemaphoreType.DMA((31,)),
            pltpu.SemaphoreType.DMA(()),
        ],
        compiler_params=pltpu.CompilerParams(
            collective_id=0, has_side_effects=True, vmem_limit_bytes=32 << 20
        ),
        name="gather_and_head_grads",
    )(*place(pltpu.HBM, q, k, v, o, lse, g, w, par, node))


def attend_kernel(plan, q4, g4, tail, kk, kt, vt, dq_in, dkv_in, dq, dkv):
    ahead = lax.broadcasted_iota(jnp.int32, (BLK, BLK), 0) - lax.broadcasted_iota(
        jnp.int32, (BLK, BLK), 1
    )

    def some(qi, first, count):
        at = [plan[0, qi * KEYS + first + u] for u in range(count)]
        at = [(i // NX, i % NX) for i in at]
        reach = jnp.where((qi == 0) & (first == 0), 0, BLK)
        join = lambda parts, dim: parts[0] if len(parts) == 1 else jnp.concatenate(parts, axis=dim)
        q_c, g_c = q4[qi], g4[qi]
        s_all = jnp.dot(join([kt[i] for i in at], 0), q_c, preferred_element_type=F32)
        dp_all = jnp.dot(join([vt[i] for i in at], 0), g_c, preferred_element_type=F32)
        w_parts, ds_parts = [], []
        for h in range(GRP):
            cols = slice(h * BLK, (h + 1) * BLK)
            p = jnp.exp2(s_all[:, cols] * (SCALE * LOG2E) - tail[qi, h : h + 1, :])
            head = jnp.where(ahead <= reach, p[:BLK], 0.0)
            p = head if count == 1 else jnp.concatenate([head, p[BLK:]], axis=0)
            w_parts.append(p.astype(BF16))
            ds_parts.append((p * (dp_all[:, cols] - tail[qi, 8 + h : 9 + h, :])).astype(BF16))
        w_all, ds_all = join(w_parts, 1), join(ds_parts, 1)
        dq[qi] += jnp.dot(join([kk[i] for i in at], 1), ds_all, preferred_element_type=F32)
        dk_t = lax.dot_general(q_c, ds_all, NT, preferred_element_type=F32)
        dv_t = lax.dot_general(g_c, w_all, NT, preferred_element_type=F32)
        for u, (zi, xi) in enumerate(at):
            dkv[zi, xi, 0] += dk_t[:, u * BLK : (u + 1) * BLK]
            dkv[zi, xi, 1] += dv_t[:, u * BLK : (u + 1) * BLK]

    def query_block(qi, carry):
        count = plan[1, qi]
        fours = (count + 1) // 4
        left = count - 4 * fours

        def four(t, carry):
            some(qi, 4 * t, 4)
            return carry

        lax.fori_loop(0, fours, four, 0)

        @pl.when(left == 2)
        def _():
            some(qi, 4 * fours, 2)

        @pl.when(left == 1)
        def _():
            some(qi, 4 * fours, 1)

        return carry

    lax.fori_loop(0, NY, query_block, 0)


def attend(plan, q4, g4, tail, kk, kt, vt, dq, dkv):
    return pl.pallas_call(
        attend_kernel,
        out_shape=(
            pltpu.VMEM((NY, HD, ROWS), F32),
            pltpu.VMEM((NZ + 1, NX, 2, HD, BLK), F32),
        ),
        in_specs=[SMEM] + [VMEM] * 8,
        out_specs=(VMEM,) * 2,
        input_output_aliases={7: 0, 8: 1},
        compiler_params=pltpu.CompilerParams(vmem_limit_bytes=32 << 20),
        name="attend_visible_pairs",
    )(plan, *place(pltpu.VMEM, q4, g4, tail, kk, kt, vt, dq, dkv))


def scatter_kernel(
    dq, dkv, qp_in, qm_in, own,
    p_out, m_out, p_in, m_in, qp_out, qm_out, q2p_out, q2m_out, qp_half, qm_half, x_out, x_in,
    unit, send_sem, recv_sems, last_sem, vouched,
):
    me = where_am_i()
    yp, ym, zp, zm, xo, xp, xm = (me[n] for n in ("yp", "ym", "zp", "zm", "xo", "xp", "xm"))
    met = hail([yp, ym, zp, zm, xo])
    wires = Wires(send_sem, recv_sems, last_sem, unit)
    send = wires.send
    got = {}
    up, down = pl.ds(0, HALF), pl.ds(HALF, HALF)
    chunks = ((1, 0, True), (1, 1, False), (1, 1, True), (1, 0, False))
    chunks += tuple((0, kv, plus) for _, kv, plus in chunks)

    def stage(left, e, kv, plus):
        slot = NZ - left if plus else left
        out, land = (p_out, p_in) if plus else (m_out, m_in)
        long = plus == (kv == 0)
        value = dkv[slot, e, kv]
        if left < (4 if long else 3):
            got[e, kv, plus]()
            value = value + land[left, e, kv].astype(F32)
        if left == 1:
            if ("x", slot) in got:
                got.pop(("x", slot))()
            got[1, kv, plus]()
            value = value + x_in[1 - plus, kv].astype(F32) + land[1, 1, kv].astype(F32)
        out[left - 1, e, kv] = value.astype(BF16)
        to = (xp if plus else xm) if (left, e) == (2, 1) else (zp if plus else zm)
        got[e, kv, plus] = send(
            out.at[left - 1, e, kv], land.at[left - 1, e, kv], to, left == 1
        )

    q2p_out[...] = dq[2, up].astype(BF16)
    q2m_out[...] = dq[2, down].astype(BF16)
    qp_out[down, :] = dq[3, down].astype(BF16)
    qm_out[up, :] = dq[1, up].astype(BF16)
    met()
    vouch(xo, vouched)
    for e, kv, plus in chunks:
        if plus == (kv == 0):
            stage(4, e, kv, plus)
    got["q2p"] = send(q2p_out, qp_half, yp)
    got["q2m"] = send(q2m_out, qm_half, ym)
    for e, kv, plus in chunks:
        if plus != (kv == 0):
            stage(3, e, kv, plus)
    send(qp_out.at[down], qp_in.at[down], yp, last=True)
    send(qm_out.at[up], qm_in.at[up], ym, last=True)
    for place, slot in enumerate((7, 1, 0)):
        x_out[place] = dkv[slot, 1].astype(BF16)
        got["x", slot] = send(x_out.at[place], x_in.at[place], xo, slot == 0)

    def turn(left):
        for e in (1, 0):
            for e2, kv, plus in chunks:
                step = left if plus == (kv == 0) else left - 1
                if e2 == e and step > e:
                    stage(step, e, kv, plus)

    pl.semaphore_wait(vouched, 1)
    turn(3)
    got["q2p"]()
    qp_out[up, :] = (dq[3, up] + qp_half[...].astype(F32)).astype(BF16)
    send(qp_out.at[up], qp_in.at[up], yp, last=True)
    got["q2m"]()
    qm_out[down, :] = (dq[1, down] + qm_half[...].astype(F32)).astype(BF16)
    send(qm_out.at[down], qm_in.at[down], ym, last=True)
    turn(2)
    turn(1)

    wires.finish(zp, sends=False)
    for kv in (0, 1):
        total = dkv[0, 0, kv] + x_in[2, kv].astype(F32)
        own[kv] = total + p_in[0, 0, kv].astype(F32) + m_in[0, 0, kv].astype(F32)
    wires.finish(zp)


def scatter(dq, dkv):
    ring = (4, NX, 2, HD, BLK)
    wide, half, pair = (HD, ROWS), (HALF, ROWS), (2, HD, BLK)
    return pl.pallas_call(
        scatter_kernel,
        out_shape=(
            pltpu.VMEM(wide, BF16),
            pltpu.VMEM(wide, BF16),
            pltpu.VMEM(pair, F32),
        ),
        in_specs=[VMEM] * 2,
        out_specs=(VMEM,) * 3,
        scratch_shapes=[pltpu.VMEM(ring, BF16)] * 4
        + [pltpu.VMEM(wide, BF16)] * 2
        + [pltpu.VMEM(half, BF16)] * 4
        + [
            pltpu.VMEM((3, *pair), BF16),
            pltpu.VMEM((3, *pair), BF16),
            pltpu.VMEM((400, 16, 128), BF16),
            pltpu.SemaphoreType.DMA(()),
            pltpu.SemaphoreType.DMA((24,)),
            pltpu.SemaphoreType.DMA(()),
            pltpu.SemaphoreType.REGULAR,
        ],
        compiler_params=pltpu.CompilerParams(
            collective_id=1, has_side_effects=True, vmem_limit_bytes=32 << 20
        ),
        name="scatter_sums",
    )(*place(pltpu.VMEM, dq, dkv))


def write_kernel(dq, qp_in, qm_in, own, q_out, k_out, v_out, q_buf, kv_buf, sems):
    copies = []
    for kv, (out, scale) in enumerate(((k_out, SCALE), (v_out, 1.0))):
        kv_buf[kv] = own[kv] * scale
        copies.append(pltpu.make_async_copy(kv_buf.at[kv], out, sems.at[kv]))
        copies[-1].start()
    for h in range(GRP):
        cols = pl.ds(h * BLK, BLK)
        total = dq[0, :, cols] + qp_in[:, cols].astype(F32) + qm_in[:, cols].astype(F32)
        q_buf[pl.ds(h * HD, HD), :] = total * SCALE
    copies.append(pltpu.make_async_copy(q_buf, q_out, sems.at[2]))
    copies[-1].start()
    for copy in copies:
        copy.wait()


def write(dq, qp_in, qm_in, own):
    return pl.pallas_call(
        write_kernel,
        out_shape=(
            jax.ShapeDtypeStruct((ROWS, BLK), F32),
            jax.ShapeDtypeStruct((HD, BLK), F32),
            jax.ShapeDtypeStruct((HD, BLK), F32),
        ),
        in_specs=[VMEM] * 4,
        out_specs=(HBM,) * 3,
        scratch_shapes=[
            pltpu.VMEM((ROWS, BLK), F32),
            pltpu.VMEM((2, HD, BLK), F32),
            pltpu.SemaphoreType.DMA((3,)),
        ],
        name="write_gradients",
    )(*place(pltpu.VMEM, dq, qp_in, qm_in, own))


def body(q, k, v, o, lse, g, w, parents, node_of):
    *rest, plan = gather(q, k, v, o, lse, g, w, parents[None, :], node_of[None, :])
    dq, dkv = attend(plan, *rest)
    return write(dq, *scatter(dq, dkv))


def solution(mesh):
    both, one = P("fsdp", "seq"), P()
    return jax.shard_map(
        body,
        mesh=mesh,
        in_specs=(both,) * 6 + (P("fsdp", None), one, one),
        out_specs=(both,) * 3,
        check_vma=False,
    )
```
